32 devices in a mesh: section: 2 (over x), tile: 16 (over z, y, core).
Axes of the slice: x: 2, y: 2, z: 4, core: 2. Of those that a mesh axis runs over, the one named last changes fastest.
Arguments:
- coarse: bfloat16 [12, 512, 128], P(None, 'tile'), may hold values from -6 to 6
- lift_weight: bfloat16 [128, 12], replicated, may hold values from -1.75 to 1.75
- conv_weight: bfloat16 [3, 3, 128, 128], replicated, may hold values from -0.1875 to 0.1875
- out_weight: bfloat16 [4, 128], replicated, may hold values from -0.5 to 0.5
- denoise_in: bfloat16 [128, 8], replicated, may hold values from -2 to 2
- denoise_mid: bfloat16 [128, 128], replicated, may hold values from -0.5 to 0.5
- denoise_out: bfloat16 [4, 128], replicated, may hold values from -0.5 to 0.5
- base_noise: bfloat16 [4, 4, 512, 128], P(None, None, 'tile'), may hold values from -5 to 5
- slot_noise: bfloat16 [4, 4, 512, 128], P(None, None, 'tile'), may hold values from -5 to 5
- extra_dest: int32 [16, 8], P('tile'), may hold values from -1 to 15, as said below
Outputs:
- moments: float32 [2, 4, 512, 128], P('section', None, 'tile')
The draws below stay inside these ranges and needn't reach their ends.
Inputs may be any that keep to these rules, and one draw needn't show every extreme that they name: `extra_dest`: the non-negative entries of row t come first and are consecutive device indices t + o, t + o + 1, ... (modulo 16) with 0 <= o and all of them within t to t + 8 - 1 modulo 16; the rest are -1. Every device is named exactly 4 times over all rows; some row has 8 non-negative entries.
All inputs are finite; a program needn't handle non-finite values.
Results may differ from the reference program's by a relative error of at most 0.0024.
Values may be sent and summed in bfloat16 or wider, within the bound.
No kernel may reach another device: no remote copies, remote signals or barrier semaphores. Data moves between devices by JAX's collectives and lax.ppermute only.
A program may use at most 64 MiB of HBM per device.

```python
import math
import jax
import jax.numpy as jnp
from jax import lax

C = 128
CIN = 12
COUT = 4
TR = 32
TC = 128
MEMB = 4
XS = 4
NSTEP = 6
EMAX = 8
NT = 16
ROWS = 512


def draw_extra_dest(key, part):
    first_key, second_key = jax.random.split(jax.random.fold_in(key, 11))
    rotation = jax.random.randint(first_key, (), 0, NT)
    shifts = jax.random.randint(second_key, (NT // 2,), 1 - XS, XS + 1)
    shifts = shifts.at[0].set(XS)
    tile_ids = jnp.arange(NT, dtype=jnp.int32)
    relative = jnp.mod(tile_ids - rotation, NT)
    pair_number = relative // 2
    leading = jnp.mod(relative, 2) == 0
    pair_start = jnp.mod(tile_ids - jnp.mod(relative, 2), NT)
    lead_count = XS + shifts[pair_number]
    member_count = jnp.where(leading, lead_count, XS - shifts[pair_number])
    member_ids = jnp.arange(EMAX, dtype=jnp.int32)
    local_slot = jnp.where(leading[:, None], member_ids[None, :], lead_count[:, None] + member_ids[None, :])
    target = jnp.mod(pair_start[:, None] + local_slot, NT)
    return jnp.where(member_ids[None, :] < member_count[:, None], target, -1).astype(jnp.int32)


def block_levels(stream_key, shape, pieces, low, high):
    factor_of = 1.0
    for axis_at, shards_of in pieces:
        draws = jax.random.uniform(jax.random.fold_in(jax.random.fold_in(stream_key, 6), axis_at), (shards_of,), jnp.float32, low / len(pieces), high / len(pieces))
        factor_of = factor_of * jnp.repeat(jnp.exp(draws), shape[axis_at] // shards_of).reshape((-1,) + (1,) * (len(shape) - 1 - axis_at))
    return factor_of


def normal_values(own_key, extent, width, reach, shards=(), kind=jnp.bfloat16):
    drawn = width * jax.random.normal(own_key, extent, jnp.float32)
    if shards:
        drawn = drawn * block_levels(own_key, extent, shards, -0.22, 0.18)
    return jnp.clip(drawn, -reach, reach).astype(kind)


def setup_inputs(seed: int = 0) -> dict:
    arg_keys = jax.random.split(jax.random.key(seed), 11)
    coarse = normal_values(arg_keys[0], (CIN, ROWS, TC), 1.0, 6.0, ((1, 16),))
    lift_weight = normal_values(arg_keys[1], (C, CIN), CIN ** -0.5, 1.75)
    conv_weight = normal_values(arg_keys[2], (3, 3, C, C), (9 * C) ** -0.5, 0.1875)
    out_weight = normal_values(arg_keys[3], (COUT, C), C ** -0.5, 0.5)
    denoise_in = normal_values(arg_keys[4], (C, 2 * COUT), (2 * COUT) ** -0.5, 2.0)
    denoise_mid = normal_values(arg_keys[5], (C, C), C ** -0.5, 0.5)
    denoise_out = normal_values(arg_keys[6], (COUT, C), C ** -0.5, 0.5)
    base_noise = normal_values(arg_keys[7], (MEMB, COUT, ROWS, TC), 1.0, 5.0, ((2, 16),))
    slot_noise = normal_values(arg_keys[8], (XS, COUT, ROWS, TC), 1.0, 5.0, ((2, 16),))
    extra_dest = draw_extra_dest(jax.random.fold_in(arg_keys[10], 71), 0)
    return {"coarse": coarse, "lift_weight": lift_weight, "conv_weight": conv_weight, "out_weight": out_weight, "denoise_in": denoise_in, "denoise_mid": denoise_mid, "denoise_out": denoise_out, "base_noise": base_noise, "slot_noise": slot_noise, "extra_dest": extra_dest}


SIGMA_MAX = 4.0
SIGMA_MIN = 0.25
PLAN_POWER = 7.0

def sigma_table(step_count):
    upper_root = SIGMA_MAX ** (1.0 / PLAN_POWER)
    lower_root = SIGMA_MIN ** (1.0 / PLAN_POWER)
    values = []
    for position in range(step_count):
        fraction = position / (step_count - 1)
        values.append((upper_root + fraction * (lower_root - upper_root)) ** PLAN_POWER)
    values.append(0.0)
    return values

def slot_sources(routes, device, slot_count):
    tile_count = routes.shape[0]
    named_here = jnp.any(routes == device, axis=1).astype(jnp.int32)
    before = (jnp.cumsum(named_here) - named_here).astype(jnp.int32)
    wanted = (before[None, :] == jnp.arange(slot_count, dtype=jnp.int32)[:, None]) & (named_here[None, :] == 1)
    tile_ids = jnp.arange(tile_count, dtype=jnp.int32)
    sources = lax.optimization_barrier(jnp.sum(jnp.where(wanted, tile_ids[None, :], 0), axis=1)).astype(jnp.int32)
    return (sources, jnp.any(wanted, axis=1))

def regress(window, lift_weight, conv_weight, out_weight):
    channels_in, height, width_cells = window.shape
    lifted = jnp.dot(lift_weight, window.reshape(channels_in, height * width_cells), preferred_element_type=jnp.float32)
    lifted = jax.nn.silu(lifted).astype(jnp.bfloat16).reshape(1, -1, height, width_cells)
    convolved = lax.conv_general_dilated(lifted.astype(jnp.float32), conv_weight.astype(jnp.float32), (1, 1), ((0, 0), (1, 1)), dimension_numbers=('NCHW', 'HWIO', 'NCHW'))
    features = jax.nn.silu(convolved[0]).astype(jnp.bfloat16)
    rows_out = height - 2
    produced = jnp.dot(out_weight, features.reshape(-1, rows_out * width_cells), preferred_element_type=jnp.float32)
    return produced.astype(jnp.bfloat16).reshape(-1, rows_out, width_cells)

def network(scaled, condition, denoise_in, denoise_mid, denoise_out):
    stacked = jnp.concatenate([scaled, condition], axis=1).astype(jnp.float32)
    first_hidden = jax.nn.silu(jnp.einsum('ci,kirw->kcrw', denoise_in.astype(jnp.float32), stacked)).astype(jnp.bfloat16)
    second_hidden = jax.nn.silu(jnp.einsum('cd,kdrw->kcrw', denoise_mid.astype(jnp.float32), first_hidden.astype(jnp.float32))).astype(jnp.bfloat16)
    return jnp.einsum('oc,kcrw->korw', denoise_out.astype(jnp.float32), second_hidden.astype(jnp.float32))

def denoise(condition, noise, denoise_in, denoise_mid, denoise_out):
    sigmas = sigma_table(NSTEP)
    latent = sigmas[0] * noise.astype(jnp.float32)
    for position in range(NSTEP):
        sigma_now = sigmas[position]
        sigma_next = sigmas[position + 1]
        input_scale = 1.0 / math.sqrt(sigma_now * sigma_now + 1.0)
        skip_scale = 1.0 / (sigma_now * sigma_now + 1.0)
        output_scale = sigma_now * input_scale
        scaled = (input_scale * latent).astype(jnp.bfloat16)
        denoised = skip_scale * latent + output_scale * network(scaled, condition, denoise_in, denoise_mid, denoise_out)
        latent = latent + (sigma_next - sigma_now) / sigma_now * (latent - denoised)
    return condition.astype(jnp.float32) + latent

def reference(coarse, lift_weight, conv_weight, out_weight, denoise_in, denoise_mid, denoise_out, base_noise, slot_noise, extra_dest):
    padded = jnp.pad(coarse, ((0, 0), (1, 1), (0, 0)))

    def regress_tile(tile_number):
        window = lax.dynamic_slice_in_dim(padded, tile_number * TR, TR + 2, 1)
        return regress(window, lift_weight, conv_weight, out_weight)
    tile_ids = jnp.arange(NT, dtype=jnp.int32)
    produced = lax.map(regress_tile, tile_ids)
    base_tiles = jnp.transpose(base_noise.reshape(MEMB, COUT, NT, TR, TC), (2, 0, 1, 3, 4))

    def base_members(inputs):
        condition, noises = inputs
        samples = denoise(jnp.broadcast_to(condition[None], noises.shape), noises, denoise_in, denoise_mid, denoise_out)
        return (lax.optimization_barrier(jnp.sum(samples, axis=0)), lax.optimization_barrier(jnp.sum(samples * samples, axis=0)))
    base_sum, base_square = lax.map(base_members, (produced, base_tiles))
    slot_tiles = jnp.transpose(slot_noise.reshape(XS, COUT, NT, TR, TC), (2, 0, 1, 3, 4))

    def slot_members(inputs):
        device, noises = inputs
        sources, slot_live = slot_sources(extra_dest, device, XS)
        samples = denoise(produced[sources], noises, denoise_in, denoise_mid, denoise_out)
        samples = jnp.where(slot_live[:, None, None, None], samples, 0.0)
        return (samples, sources)
    slot_samples, slot_from = lax.map(slot_members, (tile_ids, slot_tiles))
    flat_samples = slot_samples.reshape(NT * XS, COUT, TR, TC)
    flat_from = slot_from.reshape(NT * XS)
    extra_sum = jax.ops.segment_sum(flat_samples, flat_from, num_segments=NT)
    extra_square = jax.ops.segment_sum(flat_samples * flat_samples, flat_from, num_segments=NT)
    member_count = (MEMB + lax.optimization_barrier(jnp.sum((extra_dest >= 0).astype(jnp.int32), axis=1))).astype(jnp.float32)
    scale_back = member_count[:, None, None, None]
    ensemble_mean = (base_sum + extra_sum) / scale_back
    ensemble_var = (base_square + extra_square) / scale_back - ensemble_mean * ensemble_mean
    moments = jnp.stack([ensemble_mean, ensemble_var])
    return jnp.transpose(moments, (0, 2, 1, 3, 4)).reshape(2, COUT, NT * TR, TC)
```

```python
import functools
import math

import jax
import jax.numpy as jnp
from jax import lax
from jax.experimental import pallas as pl
from jax.experimental.pallas import tpu as pltpu
from jax.sharding import PartitionSpec as P

NSTEP = 6
SIGMA_MAX = 4.0
SIGMA_MIN = 0.25
PLAN_POWER = 7.0
SECTIONS = 2
REACH = 8
VMEM_LIMIT = 40 * 1024 * 1024


def sigma_table(step_count):
    upper_root = SIGMA_MAX ** (1.0 / PLAN_POWER)
    lower_root = SIGMA_MIN ** (1.0 / PLAN_POWER)
    values = []
    for position in range(step_count):
        fraction = position / (step_count - 1)
        values.append((upper_root + fraction * (lower_root - upper_root)) ** PLAN_POWER)
    values.append(0.0)
    return values


def step_table():
    sigmas = sigma_table(NSTEP)
    steps = []
    for now, after in zip(sigmas[:-1], sigmas[1:]):
        scale = 1.0 / math.sqrt(now * now + 1.0)
        skip = 1.0 / (now * now + 1.0)
        rate = (after - now) / now
        steps.append((scale, 1.0 + rate * (1.0 - skip), -rate * now * scale))
    return sigmas[0], steps


def half_silu(half):
    return (half * jnp.tanh(half) + half).astype(jnp.bfloat16)


def dot(left, right):
    return jnp.dot(left, right, preferred_element_type=jnp.float32)


def halved(weight):
    return (0.5 * weight.astype(jnp.float32)).astype(jnp.bfloat16)


def denoise(noise, condition, w_in, w_mid, w_out):
    start, steps = step_table()
    latent = start * noise
    for scale, keep, gain in steps:
        stacked = jnp.concatenate([(scale * latent).astype(jnp.bfloat16), condition], axis=0)
        hidden = half_silu(dot(w_in, stacked))
        hidden = half_silu(dot(w_mid, hidden))
        latent = keep * latent + gain * dot(w_out, hidden)
    return condition.astype(jnp.float32) + latent


def flat(field):
    return field.astype(jnp.float32).reshape(field.shape[0], -1)


def regress_kernel(coarse_ref, edge_ref, lift_ref, conv_ref, out_ref, condition_ref):
    section = lax.axis_index("section")
    channels_in, rows_all, width = coarse_ref.shape
    rows = rows_all // SECTIONS
    coarse = coarse_ref[...].astype(jnp.float32)
    edge = edge_ref[...].astype(jnp.float32)
    upper = jnp.concatenate([edge, coarse[:, : rows + 1]], axis=1)
    lower = jnp.concatenate([coarse[:, rows - 1 :], edge], axis=1)
    window = jnp.where(section == 0, upper, lower)
    window = window.reshape(channels_in, (rows + 2) * width).astype(jnp.bfloat16)
    half = dot(halved(lift_ref[...]), window)
    lifted = half * jnp.tanh(half) + half
    channels = lifted.shape[0]
    column = lax.broadcasted_iota(jnp.int32, (channels, width), 1)
    taps = []
    for row in range(rows + 2):
        piece = lifted[:, row * width : (row + 1) * width]
        left = jnp.where(column == 0, 0.0, pltpu.roll(piece, 1, 1))
        right = jnp.where(column == width - 1, 0.0, pltpu.roll(piece, width - 1, 1))
        taps.append(jnp.concatenate([left, piece, right], axis=0).astype(jnp.bfloat16))
    stacked = jnp.concatenate(taps, axis=1)
    half = None
    for tap in range(3):
        weight = halved(conv_ref[tap].reshape(3 * channels, channels))
        part = lax.dot_general(
            weight,
            stacked[:, tap * width : (tap + rows) * width],
            (((0,), (0,)), ((), ())),
            preferred_element_type=jnp.float32,
        )
        half = part if half is None else half + part
    condition_ref[...] = dot(out_ref[...], half_silu(half)).astype(jnp.bfloat16)


def base_kernel(noise_ref, condition_ref, in_ref, mid_ref, out_ref, sums_ref):
    section = lax.axis_index("section")
    members, channels, rows_all, width = noise_ref.shape
    rows = rows_all // SECTIONS
    condition = condition_ref[...]
    noise = []
    for member in range(members):
        upper = noise_ref[member, :, :rows]
        lower = noise_ref[member, :, rows:]
        noise.append(flat(jnp.where(section == 0, upper, lower)))
    samples = denoise(
        jnp.concatenate(noise, axis=1),
        jnp.concatenate([condition] * members, axis=1),
        halved(in_ref[...]),
        halved(mid_ref[...]),
        out_ref[...],
    )
    cells = rows * width
    pieces = [samples[:, m * cells : (m + 1) * cells] for m in range(members)]
    sums_ref[0] = functools.reduce(lambda a, b: a + b, pieces)
    sums_ref[1] = functools.reduce(lambda a, b: a + b, [p * p for p in pieces])


def slot_kernel(
    routes_ref,
    near_ref,
    far2_ref,
    far4_ref,
    far6_ref,
    far8_ref,
    mine_ref,
    theirs_ref,
    base_ref,
    in_ref,
    mid_ref,
    out_ref,
    own_ref,
    peer_ref,
    noise_ref,
    sample_ref,
    where_ref,
):
    tile = lax.axis_index("tile")
    tiles = lax.axis_size("tile")
    core = lax.rem(tile, 2)
    chip_tile = tile - core
    records = (near_ref, far2_ref, far4_ref, far6_ref, far8_ref)
    channels, cells = mine_ref.shape
    rows, width = noise_ref.shape[2:]

    def names(table, device):
        first = routes_ref[table * REACH]
        place = lax.rem(device - first + tiles, tiles)
        entry = routes_ref[table * REACH + jnp.minimum(place, REACH - 1)]
        return (first >= 0) & (place < REACH) & (entry >= 0)

    def members_of(table):
        return 4 + sum((routes_ref[table * REACH + j] >= 0).astype(jnp.int32) for j in range(REACH))

    own_row = REACH + core
    peer_row = REACH + 1 - core
    found = []
    for step in range(5):
        device_row = own_row + 2 * step
        device = lax.rem(tile + 2 * step, tiles)
        source_tiles, named = [], []
        for back in range(REACH):
            row = device_row - back
            source_tiles.append(lax.rem(chip_tile + row - REACH + tiles, tiles))
            named.append(names(row, device))
        for side, row in ((0, own_row), (1, peer_row)):
            back = device_row - row
            inside = (back >= 0) & (back < REACH)
            target = lax.rem(chip_tile + row - REACH, tiles)
            live = jnp.int32(0)
            rank = jnp.int32(0)
            for at in range(REACH):
                live = live | ((back == at) & named[at]).astype(jnp.int32)
                rank = rank + (named[at] & (source_tiles[at] < target)).astype(jnp.int32)
            found.append((step, side, inside & (live == 1), rank))

    count = jnp.int32(0)
    for step, side, live, rank in found:
        place = count

        @pl.when(live)
        def _():
            noise_ref[place] = records[step][pl.ds(channels * rank, channels)]
            where_ref[place] = side

        count = count + live.astype(jnp.int32)

    own_scale = 1.0 / members_of(own_row).astype(jnp.float32)
    peer_scale = 1.0 / members_of(peer_row).astype(jnp.float32)
    sample_ref[0] = base_ref[...]
    sample_ref[1] = jnp.zeros_like(base_ref)
    w_in, w_mid, w_out = halved(in_ref[...]), halved(mid_ref[...]), out_ref[...]
    group = 2

    @pl.loop(0, (count + group - 1) // group)
    def _(turn):
        noise, conditions, sides = [], [], []
        for member in range(group):
            place = group * turn + member
            side = where_ref[jnp.minimum(place, count - 1)]
            sides.append(side)
            noise.append(flat(noise_ref[place]))
            conditions.append(jnp.where(side == 0, mine_ref[...], theirs_ref[...]))
        samples = denoise(
            jnp.concatenate(noise, axis=1), jnp.concatenate(conditions, axis=1), w_in, w_mid, w_out
        )
        for member in range(group):
            live = group * turn + member < count
            sample = samples[:, member * cells : (member + 1) * cells]
            sample = jnp.where(live, sample, 0.0)
            sample_ref[sides[member], 0] += sample
            sample_ref[sides[member], 1] += sample * sample

    for moment in range(2):
        own_ref[moment] = (own_scale * sample_ref[0, moment]).reshape(channels, rows, width)
        peer_ref[moment] = (peer_scale * sample_ref[1, moment]).reshape(channels, rows, width)


def in_vmem(count):
    return [pl.BlockSpec(memory_space=pltpu.VMEM)] * count


def from_ahead(block, distance):
    count = lax.axis_size("tile")
    return lax.ppermute(block, "tile", [((i + distance) % count, i) for i in range(count)])


def swap_cores(block):
    count = lax.axis_size("tile")
    return lax.ppermute(block, "tile", [(i, i ^ 1) for i in range(count)])


def swap_sections(block):
    return lax.ppermute(block, "section", [(0, 1), (1, 0)])


def edge_rows(coarse, section):
    count = lax.axis_size("tile")
    pairs = [(t, t + 1) for t in range(count - 1)]
    pairs += [(count + t + 1, count + t) for t in range(count - 1)]
    last = coarse[:, -1:]
    first = coarse[:, :1]
    return lax.ppermute(jnp.where(section == 0, last, first), ("section", "tile"), pairs)


def body(
    coarse,
    lift_weight,
    conv_weight,
    out_weight,
    denoise_in,
    denoise_mid,
    denoise_out,
    base_noise,
    slot_noise,
    extra_dest,
):
    section = lax.axis_index("section")
    tile = lax.axis_index("tile")
    count = lax.axis_size("tile")
    slots, channels, rows_all, width = slot_noise.shape
    members = base_noise.shape[0]
    rows = rows_all // SECTIONS
    cells = rows * width
    hidden = denoise_mid.shape[0]
    step_flops = 2 * NSTEP * hidden * (hidden + 3 * channels)
    params = pltpu.CompilerParams(vmem_limit_bytes=VMEM_LIMIT)

    edge = edge_rows(coarse, section)
    half_noise = lax.dynamic_slice_in_dim(slot_noise, rows * section, rows, axis=2)
    half_noise = half_noise.reshape(slots * channels, rows, width)
    far8_noise = from_ahead(half_noise, 8)
    far8_routes = from_ahead(extra_dest, 8)

    condition = pl.pallas_call(
        regress_kernel,
        out_shape=jax.ShapeDtypeStruct((channels, cells), jnp.bfloat16),
        in_specs=in_vmem(5),
        out_specs=pl.BlockSpec(memory_space=pltpu.VMEM),
        compiler_params=params,
        cost_estimate=pl.CostEstimate(
            flops=2 * cells * hidden * (9 * hidden + 16),
            bytes_accessed=600_000,
            transcendentals=2 * cells * hidden,
        ),
        name="regression",
    )(coarse, edge, lift_weight, conv_weight, out_weight)

    pair = jnp.concatenate([extra_dest, far8_routes], axis=0).astype(jnp.bfloat16)
    pair = jnp.pad(pair, ((0, rows - 2), (0, width - REACH)))
    record = jnp.concatenate([half_noise, pair[None]], axis=0)
    far2, far4, far6 = [from_ahead(record, distance) for distance in (2, 4, 6)]
    got = [r[-1, :2, :REACH].astype(jnp.int32) for r in (far2, far4, far6)]
    if count == 2 * REACH:
        behind = [far8_routes[0], got[0][1], got[1][1], got[2][1]]
    else:
        behind = [from_ahead(extra_dest, -distance)[0] for distance in (8, 6, 4, 2)]
    ahead = [extra_dest[0], got[0][0], got[1][0], got[2][0], far8_routes[0]]
    own_routes = jnp.stack(behind + ahead)
    peer_condition = swap_cores(condition)
    peer_routes = swap_cores(own_routes)
    even = jnp.where(tile % 2 == 0, own_routes, peer_routes)
    odd = jnp.where(tile % 2 == 0, peer_routes, own_routes)
    routes = jnp.stack([even, odd], axis=1).reshape(-1)

    base = pl.pallas_call(
        base_kernel,
        out_shape=jax.ShapeDtypeStruct((2, channels, cells), jnp.float32),
        in_specs=in_vmem(5),
        out_specs=pl.BlockSpec(memory_space=pltpu.VMEM),
        compiler_params=params,
        cost_estimate=pl.CostEstimate(
            flops=members * cells * step_flops,
            bytes_accessed=400_000,
            transcendentals=2 * NSTEP * members * cells * hidden,
        ),
        name="base_members",
    )(base_noise, condition, denoise_in, denoise_mid, denoise_out)

    moments = jax.ShapeDtypeStruct((2, channels, rows, width), jnp.float32)
    own, peer = pl.pallas_call(
        slot_kernel,
        out_shape=(moments, moments),
        in_specs=[pl.BlockSpec(memory_space=pltpu.SMEM)] + in_vmem(11),
        out_specs=(pl.BlockSpec(memory_space=pltpu.VMEM),) * 2,
        scratch_shapes=[
            pltpu.VMEM((2 * 5, channels, rows, width), jnp.bfloat16),
            pltpu.VMEM((2, 2, channels, cells), jnp.float32),
            pltpu.SMEM((2 * 5,), jnp.int32),
        ],
        compiler_params=params,
        cost_estimate=pl.CostEstimate(
            flops=slots * cells * step_flops,
            bytes_accessed=1_000_000,
            transcendentals=2 * NSTEP * slots * cells * hidden,
        ),
        name="slot_members",
    )(
        routes,
        half_noise,
        far2,
        far4,
        far6,
        far8_noise,
        condition,
        peer_condition,
        base,
        denoise_in,
        denoise_mid,
        denoise_out,
    )
    total = own + swap_cores(peer)
    mean = total[0]
    variance = total[1] - mean * mean
    kept = jnp.where(section == 0, mean, variance)
    sent = jnp.where(section == 0, variance, mean)
    received = swap_sections(sent)
    upper = jnp.where(section == 0, kept, received)
    lower = jnp.where(section == 0, received, kept)
    return jnp.concatenate([upper, lower], axis=1)[None]


def solution(mesh):
    in_specs = (
        P(None, "tile", None),
        P(),
        P(),
        P(),
        P(),
        P(),
        P(),
        P(None, None, "tile", None),
        P(None, None, "tile", None),
        P("tile", None),
    )
    out_specs = P("section", None, "tile", None)
    return jax.shard_map(body, mesh=mesh, in_specs=in_specs, out_specs=out_specs, check_vma=False)
```

```python
import functools
import math

import jax
import jax.numpy as jnp
from jax import lax
from jax.experimental import pallas as pl
from jax.experimental.pallas import tpu as pltpu
from jax.sharding import PartitionSpec as P

NSTEP = 6
SIGMA_MAX = 4.0
SIGMA_MIN = 0.25
PLAN_POWER = 7.0
SECTIONS = 2
REACH = 8
VMEM_LIMIT = 40 * 1024 * 1024


def sigma_table(step_count):
    upper_root = SIGMA_MAX ** (1.0 / PLAN_POWER)
    lower_root = SIGMA_MIN ** (1.0 / PLAN_POWER)
    values = []
    for position in range(step_count):
        fraction = position / (step_count - 1)
        values.append((upper_root + fraction * (lower_root - upper_root)) ** PLAN_POWER)
    values.append(0.0)
    return values


def step_table():
    sigmas = sigma_table(NSTEP)
    steps = []
    for now, after in zip(sigmas[:-1], sigmas[1:]):
        scale = 1.0 / math.sqrt(now * now + 1.0)
        skip = 1.0 / (now * now + 1.0)
        rate = (after - now) / now
        steps.append((scale, 1.0 + rate * (1.0 - skip), -rate * now * scale))
    return sigmas[0], steps


def half_silu(half):
    return (half * jnp.tanh(half) + half).astype(jnp.bfloat16)


def dot(left, right):
    return jnp.dot(left, right, preferred_element_type=jnp.float32)


def dot_rows(left, right):
    return lax.dot_general(
        left, right, (((0,), (0,)), ((), ())), preferred_element_type=jnp.float32
    )


def halved(weight):
    return (0.5 * weight.astype(jnp.float32)).astype(jnp.bfloat16)


def denoise(noise, condition, w_in, w_mid, w_out):
    start, steps = step_table()
    latent = start * noise
    for scale, keep, gain in steps:
        stacked = jnp.concatenate([(scale * latent).astype(jnp.bfloat16), condition], axis=0)
        hidden = half_silu(dot_rows(w_in, stacked))
        hidden = half_silu(dot(w_mid, hidden))
        latent = keep * latent + gain * dot(w_out, hidden)
    return condition.astype(jnp.float32) + latent


def flat(field):
    return field.astype(jnp.float32).reshape(field.shape[0], -1)


def regress_kernel(
    coarse_ref,
    edge_ref,
    lift_hbm,
    conv_hbm,
    out_hbm,
    in_hbm,
    mid_hbm,
    condition_ref,
    in_ref,
    mid_ref,
    lift_ref,
    conv_ref,
    out_ref,
    sems,
):
    section = lax.axis_index("section")
    channels_in, rows_all, width = coarse_ref.shape
    rows = rows_all // SECTIONS
    pairs = (
        (lift_hbm, lift_ref),
        (conv_hbm, conv_ref),
        (out_hbm, out_ref),
        (in_hbm, in_ref),
        (mid_hbm, mid_ref),
    )
    copies = [pltpu.make_async_copy(a, b, sems.at[i]) for i, (a, b) in enumerate(pairs)]
    for copy in copies:
        copy.start()
    coarse = coarse_ref[...].astype(jnp.float32)
    edge = edge_ref[...].astype(jnp.float32)
    upper = jnp.concatenate([edge, coarse[:, : rows + 1]], axis=1)
    lower = jnp.concatenate([coarse[:, rows - 1 :], edge], axis=1)
    window = jnp.where(section == 0, upper, lower)
    window = window.reshape(channels_in, (rows + 2) * width).astype(jnp.bfloat16)
    copies[0].wait()
    half = dot_rows(halved(lift_ref[...]), window)
    lifted = half * jnp.tanh(half) + half
    channels = lifted.shape[0]
    column = lax.broadcasted_iota(jnp.int32, (channels, width), 1)
    taps = []
    for row in range(rows + 2):
        piece = lifted[:, row * width : (row + 1) * width]
        left = jnp.where(column == 0, 0.0, pltpu.roll(piece, 1, 1))
        right = jnp.where(column == width - 1, 0.0, pltpu.roll(piece, width - 1, 1))
        taps.append(jnp.concatenate([left, piece, right], axis=0).astype(jnp.bfloat16))
    stacked = jnp.concatenate(taps, axis=1)
    copies[1].wait()
    half = None
    for tap in range(3):
        weight = halved(conv_ref[tap].reshape(3 * channels, channels))
        part = dot_rows(weight, stacked[:, tap * width : (tap + rows) * width])
        half = part if half is None else half + part
    for copy in copies[2:]:
        copy.wait()
    condition_ref[...] = dot(out_ref[...], half_silu(half)).astype(jnp.bfloat16)
    in_ref[...] = halved(in_ref[...])
    mid_ref[...] = halved(mid_ref[...])


def base_kernel(noise_ref, condition_ref, in_ref, mid_ref, out_ref, sums_ref):
    section = lax.axis_index("section")
    members, channels, rows_all, width = noise_ref.shape
    rows = rows_all // SECTIONS
    condition = condition_ref[...]
    noise = []
    for member in range(members):
        upper = noise_ref[member, :, :rows]
        lower = noise_ref[member, :, rows:]
        noise.append(flat(jnp.where(section == 0, upper, lower)))
    samples = denoise(
        jnp.concatenate(noise, axis=1),
        jnp.concatenate([condition] * members, axis=1),
        in_ref[...],
        mid_ref[...],
        out_ref[...],
    )
    cells = rows * width
    pieces = [samples[:, m * cells : (m + 1) * cells] for m in range(members)]
    sums_ref[0] = functools.reduce(lambda a, b: a + b, pieces)
    sums_ref[1] = functools.reduce(lambda a, b: a + b, [p * p for p in pieces])


def slot_kernel(
    routes_ref,
    near_ref,
    far2_ref,
    far4_ref,
    far6_ref,
    far8_ref,
    mine_ref,
    theirs_ref,
    base_ref,
    in_ref,
    mid_ref,
    out_ref,
    own_ref,
    peer_ref,
    noise_ref,
    sample_ref,
    where_ref,
):
    tile = lax.axis_index("tile")
    tiles = lax.axis_size("tile")
    core = lax.rem(tile, 2)
    chip_tile = tile - core
    records = (near_ref, far2_ref, far4_ref, far6_ref, far8_ref)
    channels, cells = mine_ref.shape
    rows, width = noise_ref.shape[2:]

    def names(table, device):
        first = routes_ref[table * REACH]
        place = lax.rem(device - first + tiles, tiles)
        entry = routes_ref[table * REACH + jnp.minimum(place, REACH - 1)]
        return (first >= 0) & (place < REACH) & (entry >= 0)

    def members_of(table):
        return 4 + sum((routes_ref[table * REACH + j] >= 0).astype(jnp.int32) for j in range(REACH))

    own_row = REACH + core
    peer_row = REACH + 1 - core
    found = []
    for step in range(5):
        device_row = own_row + 2 * step
        device = lax.rem(tile + 2 * step, tiles)
        source_tiles, named = [], []
        for back in range(REACH):
            row = device_row - back
            source_tiles.append(lax.rem(chip_tile + row - REACH + tiles, tiles))
            named.append(names(row, device))
        for side, row in ((0, own_row), (1, peer_row)):
            back = device_row - row
            inside = (back >= 0) & (back < REACH)
            target = lax.rem(chip_tile + row - REACH, tiles)
            live = jnp.int32(0)
            rank = jnp.int32(0)
            for at in range(REACH):
                live = live | ((back == at) & named[at]).astype(jnp.int32)
                rank = rank + (named[at] & (source_tiles[at] < target)).astype(jnp.int32)
            found.append((step, side, inside & (live == 1), rank))

    count = jnp.int32(0)
    for step, side, live, rank in found:
        place = count

        @pl.when(live)
        def _():
            noise_ref[place] = records[step][pl.ds(channels * rank, channels)]
            where_ref[place] = side

        count = count + live.astype(jnp.int32)

    own_scale = 1.0 / members_of(own_row).astype(jnp.float32)
    peer_scale = 1.0 / members_of(peer_row).astype(jnp.float32)
    sample_ref[0] = base_ref[...]
    sample_ref[1] = jnp.zeros_like(base_ref)
    w_in, w_mid, w_out = in_ref[...], mid_ref[...], out_ref[...]

    def run(first, group):
        noise, conditions, sides = [], [], []
        for member in range(group):
            side = where_ref[jnp.minimum(first + member, count - 1)]
            sides.append(side)
            noise.append(flat(noise_ref[first + member]))
            conditions.append(jnp.where(side == 0, mine_ref[...], theirs_ref[...]))
        samples = denoise(
            jnp.concatenate(noise, axis=1), jnp.concatenate(conditions, axis=1), w_in, w_mid, w_out
        )
        for member in range(group):
            sample = samples[:, member * cells : (member + 1) * cells]
            sample = jnp.where(first + member < count, sample, 0.0)
            sample_ref[sides[member], 0] += sample
            sample_ref[sides[member], 1] += sample * sample

    fours = (count + 1) // 4

    @pl.loop(0, fours)
    def _(turn):
        run(4 * turn, 4)

    @pl.when(count > 4 * fours)
    def _():
        run(4 * fours, 2)

    for moment in range(2):
        own_ref[moment] = (own_scale * sample_ref[0, moment]).reshape(channels, rows, width)
        peer_ref[moment] = (peer_scale * sample_ref[1, moment]).reshape(channels, rows, width)


def in_vmem(count):
    return [pl.BlockSpec(memory_space=pltpu.VMEM)] * count


def from_ahead(block, distance):
    count = lax.axis_size("tile")
    return lax.ppermute(block, "tile", [((i + distance) % count, i) for i in range(count)])


def swap_cores(block):
    count = lax.axis_size("tile")
    return lax.ppermute(block, "tile", [(i, i ^ 1) for i in range(count)])


def swap_sections(block):
    return lax.ppermute(block, "section", [(0, 1), (1, 0)])


def edge_rows(coarse, section):
    count = lax.axis_size("tile")
    pairs = [(t, t + 1) for t in range(count - 1)]
    pairs += [(count + t + 1, count + t) for t in range(count - 1)]
    last = coarse[:, -1:]
    first = coarse[:, :1]
    return lax.ppermute(jnp.where(section == 0, last, first), ("section", "tile"), pairs)


def body(
    coarse,
    lift_weight,
    conv_weight,
    out_weight,
    denoise_in,
    denoise_mid,
    denoise_out,
    base_noise,
    slot_noise,
    extra_dest,
):
    section = lax.axis_index("section")
    tile = lax.axis_index("tile")
    count = lax.axis_size("tile")
    slots, channels, rows_all, width = slot_noise.shape
    members = base_noise.shape[0]
    rows = rows_all // SECTIONS
    cells = rows * width
    hidden = denoise_mid.shape[0]
    step_flops = 2 * NSTEP * hidden * (hidden + 3 * channels)
    params = pltpu.CompilerParams(vmem_limit_bytes=VMEM_LIMIT)

    edge = edge_rows(coarse, section)
    half_noise = lax.dynamic_slice_in_dim(slot_noise, rows * section, rows, axis=2)
    half_noise = half_noise.reshape(slots * channels, rows, width)

    def record_of(routes):
        block = jnp.pad(routes.astype(jnp.bfloat16), ((0, rows - routes.shape[0]), (0, width - REACH)))
        return jnp.concatenate([half_noise, block[None]], axis=0)

    far8 = from_ahead(record_of(extra_dest), 8)

    weight = jax.ShapeDtypeStruct((2 * channels, hidden), jnp.bfloat16)
    condition, w_in, w_mid = pl.pallas_call(
        regress_kernel,
        out_shape=(
            jax.ShapeDtypeStruct((channels, cells), jnp.bfloat16),
            weight,
            jax.ShapeDtypeStruct((hidden, hidden), jnp.bfloat16),
        ),
        in_specs=in_vmem(2) + [pl.BlockSpec(memory_space=pl.ANY)] * 5,
        out_specs=(pl.BlockSpec(memory_space=pltpu.VMEM),) * 3,
        scratch_shapes=[
            pltpu.VMEM((coarse.shape[0], hidden), jnp.bfloat16),
            pltpu.VMEM(conv_weight.shape, jnp.bfloat16),
            pltpu.VMEM(out_weight.shape, jnp.bfloat16),
            pltpu.SemaphoreType.DMA((5,)),
        ],
        compiler_params=params,
        cost_estimate=pl.CostEstimate(
            flops=2 * cells * hidden * (9 * hidden + 16),
            bytes_accessed=600_000,
            transcendentals=2 * cells * hidden,
        ),
        name="regression",
    )(coarse, edge, lift_weight.T, conv_weight, out_weight, denoise_in.T, denoise_mid)

    far8_after, condition = lax.optimization_barrier((far8, condition))
    far8_routes = far8_after[-1, :1, :REACH].astype(jnp.int32)
    record = record_of(jnp.concatenate([extra_dest, far8_routes], axis=0))
    far2, far4, far6 = [from_ahead(record, distance) for distance in (2, 4, 6)]
    got = [r[-1, :2, :REACH].astype(jnp.int32) for r in (far2, far4, far6)]
    if count == 2 * REACH:
        behind = [far8_routes[0], got[0][1], got[1][1], got[2][1]]
    else:
        behind = [from_ahead(extra_dest, -distance)[0] for distance in (8, 6, 4, 2)]
    ahead = [extra_dest[0], got[0][0], got[1][0], got[2][0], far8_routes[0]]
    own_routes = jnp.stack(behind + ahead)
    peer_condition = swap_cores(condition)
    peer_routes = swap_cores(own_routes)
    even = jnp.where(tile % 2 == 0, own_routes, peer_routes)
    odd = jnp.where(tile % 2 == 0, peer_routes, own_routes)
    routes = jnp.stack([even, odd], axis=1).reshape(-1)

    base = pl.pallas_call(
        base_kernel,
        out_shape=jax.ShapeDtypeStruct((2, channels, cells), jnp.float32),
        in_specs=in_vmem(5),
        out_specs=pl.BlockSpec(memory_space=pltpu.VMEM),
        compiler_params=params,
        cost_estimate=pl.CostEstimate(
            flops=members * cells * step_flops,
            bytes_accessed=400_000,
            transcendentals=2 * NSTEP * members * cells * hidden,
        ),
        name="base_members",
    )(base_noise, condition, w_in, w_mid, denoise_out)

    moments = jax.ShapeDtypeStruct((2, channels, rows, width), jnp.float32)
    own, peer = pl.pallas_call(
        slot_kernel,
        out_shape=(moments, moments),
        in_specs=[pl.BlockSpec(memory_space=pltpu.SMEM)] + in_vmem(11),
        out_specs=(pl.BlockSpec(memory_space=pltpu.VMEM),) * 2,
        scratch_shapes=[
            pltpu.VMEM((12, channels, rows, width), jnp.bfloat16),
            pltpu.VMEM((2, 2, channels, cells), jnp.float32),
            pltpu.SMEM((12,), jnp.int32),
        ],
        compiler_params=params,
        cost_estimate=pl.CostEstimate(
            flops=slots * cells * step_flops,
            bytes_accessed=1_000_000,
            transcendentals=2 * NSTEP * slots * cells * hidden,
        ),
        name="slot_members",
    )(
        routes,
        half_noise,
        far2,
        far4,
        far6,
        far8,
        condition,
        peer_condition,
        base,
        w_in,
        w_mid,
        denoise_out,
    )
    total = own + swap_cores(peer)
    mean = total[0]
    variance = total[1] - mean * mean
    kept = jnp.where(section == 0, mean, variance)
    sent = jnp.where(section == 0, variance, mean)
    received = swap_sections(sent)
    upper = jnp.where(section == 0, kept, received)
    lower = jnp.where(section == 0, received, kept)
    return jnp.concatenate([upper, lower], axis=1)[None]


def solution(mesh):
    in_specs = (
        P(None, "tile", None),
        P(),
        P(),
        P(),
        P(),
        P(),
        P(),
        P(None, None, "tile", None),
        P(None, None, "tile", None),
        P("tile", None),
    )
    out_specs = P("section", None, "tile", None)
    return jax.shard_map(body, mesh=mesh, in_specs=in_specs, out_specs=out_specs, check_vma=False)
```

```python
import functools
import math

import jax
import jax.numpy as jnp
from jax import lax
from jax.experimental import pallas as pl
from jax.experimental.pallas import tpu as pltpu
from jax.sharding import PartitionSpec as P

NSTEP = 6
SIGMA_MAX = 4.0
SIGMA_MIN = 0.25
PLAN_POWER = 7.0
SECTIONS = 2
REACH = 8
VMEM_LIMIT = 40 * 1024 * 1024


def sigma_table(step_count):
    upper_root = SIGMA_MAX ** (1.0 / PLAN_POWER)
    lower_root = SIGMA_MIN ** (1.0 / PLAN_POWER)
    values = []
    for position in range(step_count):
        fraction = position / (step_count - 1)
        values.append((upper_root + fraction * (lower_root - upper_root)) ** PLAN_POWER)
    values.append(0.0)
    return values


def step_table():
    sigmas = sigma_table(NSTEP)
    steps = []
    for now, after in zip(sigmas[:-1], sigmas[1:]):
        scale = 1.0 / math.sqrt(now * now + 1.0)
        skip = 1.0 / (now * now + 1.0)
        rate = (after - now) / now
        steps.append((scale, 1.0 + rate * (1.0 - skip), -rate * now * scale))
    return sigmas[0], steps


def half_silu(half):
    return (half * jnp.tanh(half) + half).astype(jnp.bfloat16)


def dot(left, right):
    return jnp.dot(left, right, preferred_element_type=jnp.float32)


def dot_rows(left, right):
    return lax.dot_general(
        left, right, (((0,), (0,)), ((), ())), preferred_element_type=jnp.float32
    )


def halved(weight):
    return (0.5 * weight.astype(jnp.float32)).astype(jnp.bfloat16)


def denoise(noise, condition, w_in, w_mid, w_out):
    start, steps = step_table()
    latent = start * noise
    for scale, keep, gain in steps:
        stacked = jnp.concatenate([(scale * latent).astype(jnp.bfloat16), condition], axis=0)
        hidden = half_silu(dot_rows(w_in, stacked))
        hidden = half_silu(dot(w_mid, hidden))
        latent = keep * latent + gain * dot(w_out, hidden)
    return condition.astype(jnp.float32) + latent


def flat(field):
    return field.astype(jnp.float32).reshape(field.shape[0], -1)


def regress_kernel(
    coarse_ref,
    edge_ref,
    lift_hbm,
    conv_hbm,
    out_hbm,
    in_hbm,
    mid_hbm,
    last_hbm,
    condition_ref,
    in_ref,
    mid_ref,
    last_ref,
    lift_ref,
    conv_ref,
    out_ref,
    sems,
):
    section = lax.axis_index("section")
    channels_in, rows_all, width = coarse_ref.shape
    rows = rows_all // SECTIONS
    pairs = (
        (lift_hbm, lift_ref),
        (conv_hbm, conv_ref),
        (out_hbm, out_ref),
        (in_hbm, in_ref),
        (mid_hbm, mid_ref),
        (last_hbm, last_ref),
    )
    copies = [pltpu.make_async_copy(a, b, sems.at[i]) for i, (a, b) in enumerate(pairs)]
    for copy in copies:
        copy.start()
    coarse = coarse_ref[...].astype(jnp.float32)
    edge = edge_ref[...].astype(jnp.float32)
    upper = jnp.concatenate([edge, coarse[:, : rows + 1]], axis=1)
    lower = jnp.concatenate([coarse[:, rows - 1 :], edge], axis=1)
    window = jnp.where(section == 0, upper, lower)
    window = window.reshape(channels_in, (rows + 2) * width).astype(jnp.bfloat16)
    copies[0].wait()
    half = dot_rows(halved(lift_ref[...]), window)
    lifted = half * jnp.tanh(half) + half
    channels = lifted.shape[0]
    column = lax.broadcasted_iota(jnp.int32, (channels, width), 1)
    taps = []
    for row in range(rows + 2):
        piece = lifted[:, row * width : (row + 1) * width]
        left = jnp.where(column == 0, 0.0, pltpu.roll(piece, 1, 1))
        right = jnp.where(column == width - 1, 0.0, pltpu.roll(piece, width - 1, 1))
        taps.append(jnp.concatenate([left, piece, right], axis=0).astype(jnp.bfloat16))
    stacked = jnp.concatenate(taps, axis=1)
    copies[1].wait()
    half = None
    for tap in range(3):
        weight = halved(conv_ref[tap].reshape(3 * channels, channels))
        part = dot_rows(weight, stacked[:, tap * width : (tap + rows) * width])
        half = part if half is None else half + part
    for copy in copies[2:]:
        copy.wait()
    condition_ref[...] = dot(out_ref[...], half_silu(half)).astype(jnp.bfloat16)
    in_ref[...] = halved(in_ref[...])
    mid_ref[...] = halved(mid_ref[...])


def base_kernel(noise_ref, condition_ref, in_ref, mid_ref, out_ref, sums_ref):
    section = lax.axis_index("section")
    members, channels, rows_all, width = noise_ref.shape
    rows = rows_all // SECTIONS
    condition = condition_ref[...]
    noise = []
    for member in range(members):
        upper = noise_ref[member, :, :rows]
        lower = noise_ref[member, :, rows:]
        noise.append(flat(jnp.where(section == 0, upper, lower)))
    samples = denoise(
        jnp.concatenate(noise, axis=1),
        jnp.concatenate([condition] * members, axis=1),
        in_ref[...],
        mid_ref[...],
        out_ref[...],
    )
    cells = rows * width
    pieces = [samples[:, m * cells : (m + 1) * cells] for m in range(members)]
    sums_ref[0] = functools.reduce(lambda a, b: a + b, pieces)
    sums_ref[1] = functools.reduce(lambda a, b: a + b, [p * p for p in pieces])


def slot_plan(table, tile, tiles):
    core = lax.rem(tile, 2)
    chip = lax.broadcasted_iota(jnp.int32, table.shape, 0)
    lane = lax.broadcasted_iota(jnp.int32, table.shape, 1)
    device = REACH + core + 2 * lane
    known = chip < 9
    parity = []
    for odd in range(2):
        index = 2 * chip + odd
        ids = tile - core + index - REACH
        ids = jnp.where(ids < 0, ids + tiles, ids)
        ids = jnp.where(ids >= tiles, ids - tiles, ids)
        part = table[:, odd * REACH : (odd + 1) * REACH]
        named = jnp.sum((part >= 0).astype(jnp.float32), axis=1, keepdims=True).astype(jnp.int32)
        begin = table[:, odd * REACH : odd * REACH + 1].astype(jnp.int32) - ids
        begin = jnp.where(begin < 0, begin + tiles, begin)
        behind = device - index
        hit = known & (behind >= begin) & (behind < begin + named)
        parity.append((index, ids, named, hit))
    plans = []
    for row in (REACH + core, REACH + 1 - core):
        target = tile - core + row - REACH
        live, rank, extra = 0, 0, 0
        for index, ids, named, hit in parity:
            live += (hit & (index == row)).astype(jnp.int32)
            rank += (hit & (ids < target)).astype(jnp.int32)
            extra += jnp.where((index == row) & (lane == 0), named, 0)
        live = jnp.sum(live.astype(jnp.float32), axis=0, keepdims=True)
        rank = jnp.sum(rank.astype(jnp.float32), axis=0, keepdims=True)
        weight = jnp.zeros((1, table.shape[1]), jnp.float32)
        for step in range(5):
            weight = jnp.where(lane[:1] == step, float(8**step), weight)
        packed = jnp.sum(weight * live * (rank + 1.0))
        plans.append((packed.astype(jnp.int32), jnp.sum(extra.astype(jnp.float32))))
    return plans


def slot_kernel(*refs, members, ring):
    if ring:
        behind_ref = None
    else:
        behind_ref, *refs = refs
    (
        near_ref,
        far2_ref,
        far4_ref,
        far6_ref,
        far8_ref,
        mine_ref,
        theirs_ref,
        base_ref,
        in_ref,
        mid_ref,
        out_ref,
        own_ref,
        peer_ref,
        noise_ref,
        sample_ref,
        where_ref,
    ) = refs
    records = (near_ref, far2_ref, far4_ref, far6_ref, far8_ref)
    blocks = [record[record.shape[0] - 1].astype(jnp.float32) for record in records]
    ahead = [block[0:1] for block in blocks]
    if ring:
        behind = [ahead[4]] + [block[1:2] for block in blocks[1:4]]
    else:
        behind = [behind_ref[0:4].astype(jnp.float32)]
    spare = jnp.full((7, near_ref.shape[2]), -1.0, jnp.float32)
    table = jnp.concatenate(behind + ahead + [spare], axis=0)
    plans = slot_plan(table, lax.axis_index("tile"), lax.axis_size("tile"))
    channels, cells = mine_ref.shape
    rows, width = noise_ref.shape[2:]
    count = jnp.int32(0)
    for side, (packed, _) in enumerate(plans):
        for step, record in enumerate(records):
            digit = lax.shift_right_logical(packed, 3 * step) & 7
            place = count

            @pl.when(digit > 0)
            def _():
                noise_ref[place] = record[pl.ds(channels * (digit - 1), channels)]
                where_ref[place] = side

            count = count + (digit > 0).astype(jnp.int32)

    own_scale, peer_scale = [1.0 / (members + extra) for _, extra in plans]
    sample_ref[0] = base_ref[...]
    sample_ref[1] = jnp.zeros_like(base_ref)
    w_in, w_mid, w_out = in_ref[...], mid_ref[...], out_ref[...]

    def run(first, group):
        noise, conditions, sides = [], [], []
        for member in range(group):
            side = where_ref[jnp.minimum(first + member, count - 1)]
            sides.append(side)
            noise.append(flat(noise_ref[first + member]))
            conditions.append(jnp.where(side == 0, mine_ref[...], theirs_ref[...]))
        samples = denoise(
            jnp.concatenate(noise, axis=1), jnp.concatenate(conditions, axis=1), w_in, w_mid, w_out
        )
        for member in range(group):
            sample = samples[:, member * cells : (member + 1) * cells]
            sample = jnp.where(first + member < count, sample, 0.0)
            sample_ref[sides[member], 0] += sample
            sample_ref[sides[member], 1] += sample * sample

    fours = (count + 1) // 4

    @pl.loop(0, fours)
    def _(turn):
        run(4 * turn, 4)

    @pl.when(count > 4 * fours)
    def _():
        run(4 * fours, 2)

    for moment in range(2):
        own_ref[moment] = (own_scale * sample_ref[0, moment]).reshape(channels, rows, width)
        peer_ref[moment] = (peer_scale * sample_ref[1, moment]).reshape(channels, rows, width)


def in_vmem(count):
    return [pl.BlockSpec(memory_space=pltpu.VMEM)] * count


def from_ahead(block, distance):
    count = lax.axis_size("tile")
    return lax.ppermute(block, "tile", [((i + distance) % count, i) for i in range(count)])


def swap_cores(block):
    count = lax.axis_size("tile")
    return lax.ppermute(block, "tile", [(i, i ^ 1) for i in range(count)])


def swap_sections(block):
    return lax.ppermute(block, "section", [(0, 1), (1, 0)])


def edge_rows(coarse, section):
    count = lax.axis_size("tile")
    pairs = [(t, t + 1) for t in range(count - 1)]
    pairs += [(count + t + 1, count + t) for t in range(count - 1)]
    last = coarse[:, -1:]
    first = coarse[:, :1]
    return lax.ppermute(jnp.where(section == 0, last, first), ("section", "tile"), pairs)


def body(
    coarse,
    lift_weight,
    conv_weight,
    out_weight,
    denoise_in,
    denoise_mid,
    denoise_out,
    base_noise,
    slot_noise,
    extra_dest,
):
    section = lax.axis_index("section")
    tile = lax.axis_index("tile")
    count = lax.axis_size("tile")
    slots, channels, rows_all, width = slot_noise.shape
    members = base_noise.shape[0]
    rows = rows_all // SECTIONS
    cells = rows * width
    hidden = denoise_mid.shape[0]
    step_flops = 2 * NSTEP * hidden * (hidden + 3 * channels)
    params = pltpu.CompilerParams(vmem_limit_bytes=VMEM_LIMIT)

    peer_routes = swap_cores(extra_dest)
    even = jnp.where(tile % 2 == 0, extra_dest, peer_routes)
    odd = jnp.where(tile % 2 == 0, peer_routes, extra_dest)
    chip_routes = jnp.concatenate([even, odd], axis=1)
    edge = edge_rows(coarse, section)
    half_noise = lax.dynamic_slice_in_dim(slot_noise, rows * section, rows, axis=2)
    half_noise = half_noise.reshape(slots * channels, rows, width)

    def record_of(routes):
        pads = ((0, rows - routes.shape[0]), (0, width - 2 * REACH))
        block = jnp.pad(routes.astype(jnp.bfloat16), pads)
        return jnp.concatenate([half_noise, block[None]], axis=0)

    def routes_of(record, row):
        return record[-1, row : row + 1, : 2 * REACH].astype(jnp.int32)

    far8 = from_ahead(record_of(chip_routes), 8)

    weight = jax.ShapeDtypeStruct((2 * channels, hidden), jnp.bfloat16)
    condition, w_in, w_mid, w_out = pl.pallas_call(
        regress_kernel,
        out_shape=(
            jax.ShapeDtypeStruct((channels, cells), jnp.bfloat16),
            weight,
            jax.ShapeDtypeStruct(denoise_mid.shape, jnp.bfloat16),
            jax.ShapeDtypeStruct(denoise_out.shape, jnp.bfloat16),
        ),
        in_specs=in_vmem(2) + [pl.BlockSpec(memory_space=pltpu.HBM)] * 6,
        out_specs=(pl.BlockSpec(memory_space=pltpu.VMEM),) * 4,
        scratch_shapes=[
            pltpu.VMEM((coarse.shape[0], hidden), jnp.bfloat16),
            pltpu.VMEM(conv_weight.shape, jnp.bfloat16),
            pltpu.VMEM(out_weight.shape, jnp.bfloat16),
            pltpu.SemaphoreType.DMA((6,)),
        ],
        compiler_params=params,
        cost_estimate=pl.CostEstimate(
            flops=2 * cells * hidden * (9 * hidden + 16),
            bytes_accessed=600_000,
            transcendentals=2 * cells * hidden,
        ),
        name="regression",
    )(coarse, edge, lift_weight.T, conv_weight, out_weight, denoise_in.T, denoise_mid, denoise_out)

    far8_after, condition = lax.optimization_barrier((far8, condition))
    record = record_of(jnp.concatenate([chip_routes, routes_of(far8_after, 0)], axis=0))
    far2, far4, far6 = [from_ahead(record, distance) for distance in (2, 4, 6)]
    peer_condition = swap_cores(condition)
    ring = count == 2 * REACH
    behind = []
    if not ring:
        block = [from_ahead(chip_routes, -distance) for distance in (8, 6, 4, 2)]
        block = jnp.concatenate(block, axis=0).astype(jnp.bfloat16)
        behind = [jnp.pad(block, ((0, rows - 4), (0, width - 2 * REACH)))]

    base = pl.pallas_call(
        base_kernel,
        out_shape=jax.ShapeDtypeStruct((2, channels, cells), jnp.float32),
        in_specs=in_vmem(5),
        out_specs=pl.BlockSpec(memory_space=pltpu.VMEM),
        compiler_params=params,
        cost_estimate=pl.CostEstimate(
            flops=members * cells * step_flops,
            bytes_accessed=400_000,
            transcendentals=2 * NSTEP * members * cells * hidden,
        ),
        name="base_members",
    )(base_noise, condition, w_in, w_mid, w_out)

    moments = jax.ShapeDtypeStruct((2, channels, rows, width), jnp.float32)
    own, peer = pl.pallas_call(
        functools.partial(slot_kernel, members=members, ring=ring),
        out_shape=(moments, moments),
        in_specs=in_vmem(11 + len(behind)),
        out_specs=(pl.BlockSpec(memory_space=pltpu.VMEM),) * 2,
        scratch_shapes=[
            pltpu.VMEM((12, channels, rows, width), jnp.bfloat16),
            pltpu.VMEM((2, 2, channels, cells), jnp.float32),
            pltpu.SMEM((12,), jnp.int32),
        ],
        compiler_params=params,
        cost_estimate=pl.CostEstimate(
            flops=slots * cells * step_flops,
            bytes_accessed=1_000_000,
            transcendentals=2 * NSTEP * slots * cells * hidden,
        ),
        name="slot_members",
    )(
        *behind,
        record,
        far2,
        far4,
        far6,
        far8,
        condition,
        peer_condition,
        base,
        w_in,
        w_mid,
        w_out,
    )
    total = own + swap_cores(peer)
    mean = total[0]
    variance = total[1] - mean * mean
    kept = jnp.where(section == 0, mean, variance)
    sent = jnp.where(section == 0, variance, mean)
    received = swap_sections(sent)
    upper = jnp.where(section == 0, kept, received)
    lower = jnp.where(section == 0, received, kept)
    return jnp.concatenate([upper, lower], axis=1)[None]


def solution(mesh):
    in_specs = (
        P(None, "tile", None),
        P(),
        P(),
        P(),
        P(),
        P(),
        P(),
        P(None, None, "tile", None),
        P(None, None, "tile", None),
        P("tile", None),
    )
    out_specs = P("section", None, "tile", None)
    return jax.shard_map(body, mesh=mesh, in_specs=in_specs, out_specs=out_specs, check_vma=False)
```

```python
import functools
import math

import jax
import jax.numpy as jnp
from jax import lax
from jax.experimental import pallas as pl
from jax.experimental.pallas import tpu as pltpu
from jax.sharding import PartitionSpec as P

NSTEP = 6
SIGMA_MAX = 4.0
SIGMA_MIN = 0.25
PLAN_POWER = 7.0
SECTIONS = 2
REACH = 8
VMEM_LIMIT = 40 * 1024 * 1024


def sigma_table(step_count):
    upper_root = SIGMA_MAX ** (1.0 / PLAN_POWER)
    lower_root = SIGMA_MIN ** (1.0 / PLAN_POWER)
    values = []
    for position in range(step_count):
        fraction = position / (step_count - 1)
        values.append((upper_root + fraction * (lower_root - upper_root)) ** PLAN_POWER)
    values.append(0.0)
    return values


def step_table():
    sigmas = sigma_table(NSTEP)
    steps = []
    for now, after in zip(sigmas[:-1], sigmas[1:]):
        scale = 1.0 / math.sqrt(now * now + 1.0)
        skip = 1.0 / (now * now + 1.0)
        rate = (after - now) / now
        steps.append((scale, 1.0 + rate * (1.0 - skip), -rate * now * scale))
    return sigmas[0], steps


def half_silu(half):
    return (half * jnp.tanh(half) + half).astype(jnp.bfloat16)


def dot(left, right):
    return jnp.dot(left, right, preferred_element_type=jnp.float32)


def halved(weight):
    return (0.5 * weight.astype(jnp.float32)).astype(jnp.bfloat16)


def dot_rows(left, right):
    return lax.dot_general(
        left, right, (((0,), (0,)), ((), ())), preferred_element_type=jnp.float32
    )


def denoise(noise, condition, w_in, w_mid, w_out):
    start, steps = step_table()
    latent = start * noise
    for scale, keep, gain in steps:
        stacked = jnp.concatenate([(scale * latent).astype(jnp.bfloat16), condition], axis=0)
        hidden = half_silu(dot_rows(w_in, stacked))
        hidden = half_silu(dot(w_mid, hidden))
        latent = keep * latent + gain * dot(w_out, hidden)
    return condition.astype(jnp.float32) + latent


def flat(field):
    return field.astype(jnp.float32).reshape(field.shape[0], -1)


def regress_kernel(
    coarse_ref,
    edge_ref,
    lift_hbm,
    conv_ref,
    out_ref,
    in_hbm,
    mid_hbm,
    last_hbm,
    condition_ref,
    in_ref,
    mid_ref,
    last_ref,
    lift_ref,
    sems,
):
    section = lax.axis_index("section")
    channels_in, rows_all, width = coarse_ref.shape
    rows = rows_all // SECTIONS
    pairs = (
        (lift_hbm, lift_ref),
        (in_hbm, in_ref),
        (mid_hbm, mid_ref),
        (last_hbm, last_ref),
    )
    copies = [pltpu.make_async_copy(a, b, sems.at[i]) for i, (a, b) in enumerate(pairs)]
    for copy in copies:
        copy.start()
    coarse = coarse_ref[...].astype(jnp.float32)
    edge = edge_ref[...].astype(jnp.float32)
    upper = jnp.concatenate([edge, coarse[:, : rows + 1]], axis=1)
    lower = jnp.concatenate([coarse[:, rows - 1 :], edge], axis=1)
    window = jnp.where(section == 0, upper, lower)
    window = window.reshape(channels_in, (rows + 2) * width).astype(jnp.bfloat16)
    copies[0].wait()
    half = dot_rows(halved(lift_ref[...]), window)
    lifted = half * jnp.tanh(half) + half
    channels = lifted.shape[0]
    column = lax.broadcasted_iota(jnp.int32, (channels, width), 1)
    taps = []
    for row in range(rows + 2):
        piece = lifted[:, row * width : (row + 1) * width]
        left = jnp.where(column == 0, 0.0, pltpu.roll(piece, 1, 1))
        right = jnp.where(column == width - 1, 0.0, pltpu.roll(piece, width - 1, 1))
        taps.append(jnp.concatenate([left, piece, right], axis=0).astype(jnp.bfloat16))
    stacked = jnp.concatenate(taps, axis=1)
    half = None
    for tap in range(3):
        weight = conv_ref[tap].reshape(3 * channels, channels)
        part = dot_rows(weight, stacked[:, tap * width : (tap + rows) * width])
        half = part if half is None else half + part
    for copy in copies[1:]:
        copy.wait()
    condition_ref[...] = (2.0 * dot(out_ref[...], half_silu(half))).astype(jnp.bfloat16)
    in_ref[...] = halved(in_ref[...])
    mid_ref[...] = halved(mid_ref[...])


def base_kernel(noise_ref, condition_ref, in_ref, mid_ref, out_ref, sums_ref):
    section = lax.axis_index("section")
    members, channels, rows_all, width = noise_ref.shape
    rows = rows_all // SECTIONS
    condition = condition_ref[...]
    noise = []
    for member in range(members):
        upper = noise_ref[member, :, :rows]
        lower = noise_ref[member, :, rows:]
        noise.append(flat(jnp.where(section == 0, upper, lower)))
    samples = denoise(
        jnp.concatenate(noise, axis=1),
        jnp.concatenate([condition] * members, axis=1),
        in_ref[...],
        mid_ref[...],
        out_ref[...],
    )
    cells = rows * width
    pieces = [samples[:, m * cells : (m + 1) * cells] for m in range(members)]
    sums_ref[0] = functools.reduce(lambda a, b: a + b, pieces)
    sums_ref[1] = functools.reduce(lambda a, b: a + b, [p * p for p in pieces])


def slot_plan(table, tile, tiles):
    core = lax.rem(tile, 2)
    chip = lax.broadcasted_iota(jnp.int32, table.shape, 0)
    lane = lax.broadcasted_iota(jnp.int32, table.shape, 1)
    device = REACH + core + 2 * lane
    known = chip < 9
    parity = []
    for odd in range(2):
        index = 2 * chip + odd
        ids = tile - core + index - REACH
        ids = jnp.where(ids < 0, ids + tiles, ids)
        ids = jnp.where(ids >= tiles, ids - tiles, ids)
        part = table[:, odd * REACH : (odd + 1) * REACH]
        named = jnp.sum((part >= 0).astype(jnp.float32), axis=1, keepdims=True).astype(jnp.int32)
        begin = table[:, odd * REACH : odd * REACH + 1].astype(jnp.int32) - ids
        begin = jnp.where(begin < 0, begin + tiles, begin)
        behind = device - index
        hit = known & (behind >= begin) & (behind < begin + named)
        parity.append((index, ids, named, hit))
    plans = []
    for row in (REACH + core, REACH + 1 - core):
        target = tile - core + row - REACH
        live, rank, extra = 0, 0, 0
        for index, ids, named, hit in parity:
            live += (hit & (index == row)).astype(jnp.int32)
            rank += (hit & (ids < target)).astype(jnp.int32)
            extra += jnp.where((index == row) & (lane == 0), named, 0)
        live = jnp.sum(live.astype(jnp.float32), axis=0, keepdims=True)
        rank = jnp.sum(rank.astype(jnp.float32), axis=0, keepdims=True)
        weight = jnp.zeros((1, table.shape[1]), jnp.float32)
        for step in range(5):
            weight = jnp.where(lane[:1] == step, float(8**step), weight)
        packed = jnp.sum(weight * live * (rank + 1.0))
        plans.append((packed.astype(jnp.int32), jnp.sum(extra.astype(jnp.float32))))
    return plans


def slot_kernel(*refs, members, ring):
    if ring:
        behind_ref = None
    else:
        behind_ref, *refs = refs
    (
        near_ref,
        far2_ref,
        far4_ref,
        far6_ref,
        far8_ref,
        mine_ref,
        theirs_ref,
        base_ref,
        in_ref,
        mid_ref,
        out_ref,
        own_ref,
        peer_ref,
        noise_ref,
        sample_ref,
        where_ref,
    ) = refs
    records = (near_ref, far2_ref, far4_ref, far6_ref, far8_ref)
    blocks = [record[record.shape[0] - 1].astype(jnp.float32) for record in records]
    ahead = [block[0:1] for block in blocks]
    if ring:
        behind = [ahead[4]] + [block[1:2] for block in blocks[1:4]]
    else:
        behind = [behind_ref[0:4].astype(jnp.float32)]
    spare = jnp.full((7, near_ref.shape[2]), -1.0, jnp.float32)
    table = jnp.concatenate(behind + ahead + [spare], axis=0)
    plans = slot_plan(table, lax.axis_index("tile"), lax.axis_size("tile"))
    channels, cells = mine_ref.shape
    rows, width = noise_ref.shape[2:]
    count = jnp.int32(0)
    for side, (packed, _) in enumerate(plans):
        for step, record in enumerate(records):
            digit = lax.shift_right_logical(packed, 3 * step) & 7
            place = count

            @pl.when(digit > 0)
            def _():
                noise_ref[place] = record[pl.ds(channels * (digit - 1), channels)]
                where_ref[place] = side

            count = count + (digit > 0).astype(jnp.int32)

    own_scale, peer_scale = [1.0 / (members + extra) for _, extra in plans]
    sample_ref[0] = base_ref[...]
    sample_ref[1] = jnp.zeros_like(base_ref)
    w_in, w_mid, w_out = in_ref[...], mid_ref[...], out_ref[...]

    def run(first, group):
        noise, conditions, sides = [], [], []
        for member in range(group):
            side = where_ref[first + member]
            sides.append(side)
            noise.append(flat(noise_ref[first + member]))
            conditions.append(jnp.where(side == 0, mine_ref[...], theirs_ref[...]))
        samples = denoise(
            jnp.concatenate(noise, axis=1), jnp.concatenate(conditions, axis=1), w_in, w_mid, w_out
        )
        for member in range(group):
            sample = samples[:, member * cells : (member + 1) * cells]
            sample_ref[sides[member], 0] += sample
            sample_ref[sides[member], 1] += sample * sample

    fours = count // 4
    left = count - 4 * fours

    @pl.loop(0, fours)
    def _(turn):
        run(4 * turn, 4)

    @pl.when(left >= 2)
    def _():
        run(4 * fours, 2)

    @pl.when((left & 1) == 1)
    def _():
        run(count - 1, 1)

    for moment in range(2):
        own_ref[moment] = (own_scale * sample_ref[0, moment]).reshape(channels, rows, width)
        peer_ref[moment] = (peer_scale * sample_ref[1, moment]).reshape(channels, rows, width)


def in_vmem(count):
    return [pl.BlockSpec(memory_space=pltpu.VMEM)] * count


def from_ahead(block, distance):
    count = lax.axis_size("tile")
    return lax.ppermute(block, "tile", [((i + distance) % count, i) for i in range(count)])


def swap_cores(block):
    count = lax.axis_size("tile")
    return lax.ppermute(block, "tile", [(i, i ^ 1) for i in range(count)])


def swap_sections(block):
    return lax.ppermute(block, "section", [(0, 1), (1, 0)])


def send_edges(rows):
    count = lax.axis_size("tile")
    pairs = [(t, t + 1) for t in range(count - 1)]
    pairs += [(count + t + 1, count + t) for t in range(count - 1)]
    return lax.ppermute(rows, ("section", "tile"), pairs)


def body(
    coarse,
    lift_weight,
    conv_weight,
    out_weight,
    denoise_in,
    denoise_mid,
    denoise_out,
    base_noise,
    slot_noise,
    extra_dest,
):
    section = lax.axis_index("section")
    tile = lax.axis_index("tile")
    count = lax.axis_size("tile")
    slots, channels, rows_all, width = slot_noise.shape
    members = base_noise.shape[0]
    rows = rows_all // SECTIONS
    cells = rows * width
    hidden = denoise_mid.shape[0]
    step_flops = 2 * NSTEP * hidden * (hidden + 3 * channels)
    params = pltpu.CompilerParams(vmem_limit_bytes=VMEM_LIMIT)

    edge = jnp.where(section == 0, coarse[:, -1:], coarse[:, :1])
    edge, extra_dest, conv_weight, out_weight = lax.optimization_barrier(
        (edge, extra_dest, conv_weight, out_weight)
    )
    edge = send_edges(edge)
    half_conv, half_out = halved(conv_weight), halved(out_weight)
    peer_routes = swap_cores(extra_dest)
    even = jnp.where(tile % 2 == 0, extra_dest, peer_routes)
    odd = jnp.where(tile % 2 == 0, peer_routes, extra_dest)
    chip_routes = jnp.concatenate([even, odd], axis=1)
    half_noise = lax.dynamic_slice_in_dim(slot_noise, rows * section, rows, axis=2)
    half_noise = half_noise.reshape(slots * channels, rows, width)

    def record_of(routes):
        pads = ((0, rows - routes.shape[0]), (0, width - 2 * REACH))
        block = jnp.pad(routes.astype(jnp.bfloat16), pads)
        return jnp.concatenate([half_noise, block[None]], axis=0)

    def routes_of(record, row):
        return record[-1, row : row + 1, : 2 * REACH].astype(jnp.int32)

    far8 = from_ahead(record_of(chip_routes), 8)

    weight = jax.ShapeDtypeStruct((2 * channels, hidden), jnp.bfloat16)
    condition, w_in, w_mid, w_out = pl.pallas_call(
        regress_kernel,
        out_shape=(
            jax.ShapeDtypeStruct((channels, cells), jnp.bfloat16),
            weight,
            jax.ShapeDtypeStruct(denoise_mid.shape, jnp.bfloat16),
            jax.ShapeDtypeStruct(denoise_out.shape, jnp.bfloat16),
        ),
        in_specs=in_vmem(2) + [pl.BlockSpec(memory_space=pl.ANY)] + in_vmem(2) + [pl.BlockSpec(memory_space=pl.ANY)] * 3,
        out_specs=(pl.BlockSpec(memory_space=pltpu.VMEM),) * 4,
        scratch_shapes=[
            pltpu.VMEM((coarse.shape[0], hidden), jnp.bfloat16),
            pltpu.SemaphoreType.DMA((4,)),
        ],
        compiler_params=params,
        cost_estimate=pl.CostEstimate(
            flops=2 * cells * hidden * (9 * hidden + 16),
            bytes_accessed=600_000,
            transcendentals=2 * cells * hidden,
        ),
        name="regression",
    )(coarse, edge, lift_weight.T, half_conv, half_out, denoise_in.T, denoise_mid, denoise_out)

    far8_after, condition = lax.optimization_barrier((far8, condition))
    record = record_of(jnp.concatenate([chip_routes, routes_of(far8_after, 0)], axis=0))
    far2, far4, far6 = [from_ahead(record, distance) for distance in (2, 4, 6)]
    peer_condition = swap_cores(condition)
    ring = count == 2 * REACH
    behind = []
    if not ring:
        block = [from_ahead(chip_routes, -distance) for distance in (8, 6, 4, 2)]
        block = jnp.concatenate(block, axis=0).astype(jnp.bfloat16)
        behind = [jnp.pad(block, ((0, rows - 4), (0, width - 2 * REACH)))]

    base = pl.pallas_call(
        base_kernel,
        out_shape=jax.ShapeDtypeStruct((2, channels, cells), jnp.float32),
        in_specs=in_vmem(5),
        out_specs=pl.BlockSpec(memory_space=pltpu.VMEM),
        compiler_params=params,
        cost_estimate=pl.CostEstimate(
            flops=members * cells * step_flops,
            bytes_accessed=400_000,
            transcendentals=2 * NSTEP * members * cells * hidden,
        ),
        name="base_members",
    )(base_noise, condition, w_in, w_mid, w_out)

    moments = jax.ShapeDtypeStruct((2, channels, rows, width), jnp.float32)
    own, peer = pl.pallas_call(
        functools.partial(slot_kernel, members=members, ring=ring),
        out_shape=(moments, moments),
        in_specs=in_vmem(11 + len(behind)),
        out_specs=(pl.BlockSpec(memory_space=pltpu.VMEM),) * 2,
        scratch_shapes=[
            pltpu.VMEM((12, channels, rows, width), jnp.bfloat16),
            pltpu.VMEM((2, 2, channels, cells), jnp.float32),
            pltpu.SMEM((12,), jnp.int32),
        ],
        compiler_params=params,
        cost_estimate=pl.CostEstimate(
            flops=slots * cells * step_flops,
            bytes_accessed=1_000_000,
            transcendentals=2 * NSTEP * slots * cells * hidden,
        ),
        name="slot_members",
    )(
        *behind,
        record,
        far2,
        far4,
        far6,
        far8,
        condition,
        peer_condition,
        base,
        w_in,
        w_mid,
        w_out,
    )
    total = own + swap_cores(peer)
    mean = total[0]
    variance = total[1] - mean * mean
    kept = jnp.where(section == 0, mean, variance)
    sent = jnp.where(section == 0, variance, mean)
    received = swap_sections(sent)
    upper = jnp.where(section == 0, kept, received)
    lower = jnp.where(section == 0, received, kept)
    return jnp.concatenate([upper, lower], axis=1)[None]


def solution(mesh):
    in_specs = (
        P(None, "tile", None),
        P(),
        P(),
        P(),
        P(),
        P(),
        P(),
        P(None, None, "tile", None),
        P(None, None, "tile", None),
        P("tile", None),
    )
    out_specs = P("section", None, "tile", None)
    return jax.shard_map(body, mesh=mesh, in_specs=in_specs, out_specs=out_specs, check_vma=False)
```

```python
import functools
import math

import jax
import jax.numpy as jnp
from jax import lax
from jax.experimental import pallas as pl
from jax.experimental.pallas import tpu as pltpu
from jax.sharding import PartitionSpec as P

NSTEP = 6
SIGMA_MAX = 4.0
SIGMA_MIN = 0.25
PLAN_POWER = 7.0
SECTIONS = 2
REACH = 8
VMEM_LIMIT = 40 * 1024 * 1024


def sigma_table(step_count):
    upper_root = SIGMA_MAX ** (1.0 / PLAN_POWER)
    lower_root = SIGMA_MIN ** (1.0 / PLAN_POWER)
    values = []
    for position in range(step_count):
        fraction = position / (step_count - 1)
        values.append((upper_root + fraction * (lower_root - upper_root)) ** PLAN_POWER)
    values.append(0.0)
    return values


def step_table():
    sigmas = sigma_table(NSTEP)
    steps = []
    for now, after in zip(sigmas[:-1], sigmas[1:]):
        scale = 1.0 / math.sqrt(now * now + 1.0)
        skip = 1.0 / (now * now + 1.0)
        rate = (after - now) / now
        steps.append((scale, 1.0 + rate * (1.0 - skip), -rate * now * scale))
    return sigmas[0], steps


def half_silu(half):
    return (half * jnp.tanh(half) + half).astype(jnp.bfloat16)


def dot(left, right):
    return jnp.dot(left, right, preferred_element_type=jnp.float32)


def halved(weight):
    return (0.5 * weight.astype(jnp.float32)).astype(jnp.bfloat16)


def dot_rows(left, right):
    return lax.dot_general(
        left, right, (((0,), (0,)), ((), ())), preferred_element_type=jnp.float32
    )


def denoise(noise, condition, w_in, w_mid, w_out):
    start, steps = step_table()
    latent = start * noise
    for scale, keep, gain in steps:
        stacked = jnp.concatenate([(scale * latent).astype(jnp.bfloat16), condition], axis=0)
        hidden = half_silu(dot_rows(w_in, stacked))
        hidden = half_silu(dot(w_mid, hidden))
        latent = keep * latent + gain * dot(w_out, hidden)
    return condition.astype(jnp.float32) + latent


def flat(field):
    return field.astype(jnp.float32).reshape(field.shape[0], -1)


def regress_kernel(
    coarse_ref,
    edge_ref,
    lift_hbm,
    conv_ref,
    ends_ref,
    in_hbm,
    mid_hbm,
    condition_ref,
    in_ref,
    mid_ref,
    last_ref,
    lift_ref,
    sems,
):
    section = lax.axis_index("section")
    channels_in, rows_all, width = coarse_ref.shape
    rows = rows_all // SECTIONS
    pairs = (
        (lift_hbm, lift_ref),
        (in_hbm, in_ref),
        (mid_hbm, mid_ref),
    )
    copies = [pltpu.make_async_copy(a, b, sems.at[i]) for i, (a, b) in enumerate(pairs)]
    for copy in copies:
        copy.start()
    coarse = coarse_ref[...].astype(jnp.float32)
    edge = edge_ref[...].astype(jnp.float32)
    upper = jnp.concatenate([edge, coarse[:, : rows + 1]], axis=1)
    lower = jnp.concatenate([coarse[:, rows - 1 :], edge], axis=1)
    window = jnp.where(section == 0, upper, lower)
    window = window.reshape(channels_in, (rows + 2) * width).astype(jnp.bfloat16)
    copies[0].wait()
    half = dot_rows(halved(lift_ref[...]), window)
    lifted = half * jnp.tanh(half) + half
    channels = lifted.shape[0]
    column = lax.broadcasted_iota(jnp.int32, (channels, width), 1)
    taps = []
    for row in range(rows + 2):
        piece = lifted[:, row * width : (row + 1) * width]
        left = jnp.where(column == 0, 0.0, pltpu.roll(piece, 1, 1))
        right = jnp.where(column == width - 1, 0.0, pltpu.roll(piece, width - 1, 1))
        taps.append(jnp.concatenate([left, piece, right], axis=0).astype(jnp.bfloat16))
    stacked = jnp.concatenate(taps, axis=1)
    half = None
    for tap in range(3):
        weight = conv_ref[tap].reshape(3 * channels, channels)
        part = dot_rows(weight, stacked[:, tap * width : (tap + rows) * width])
        half = part if half is None else half + part
    for copy in copies[1:]:
        copy.wait()
    ends = 2.0 * ends_ref[...].astype(jnp.float32)
    last_ref[...] = ends[ends.shape[0] // 2 :].astype(jnp.bfloat16)
    out_weight = ends[: ends.shape[0] // 2].astype(jnp.bfloat16)
    condition_ref[...] = dot(out_weight, half_silu(half)).astype(jnp.bfloat16)
    in_ref[...] = halved(in_ref[...])
    mid_ref[...] = halved(mid_ref[...])


def base_kernel(noise_ref, condition_ref, in_ref, mid_ref, out_ref, sums_ref):
    section = lax.axis_index("section")
    members, channels, rows_all, width = noise_ref.shape
    rows = rows_all // SECTIONS
    condition = condition_ref[...]
    noise = []
    for member in range(members):
        upper = noise_ref[member, :, :rows]
        lower = noise_ref[member, :, rows:]
        noise.append(flat(jnp.where(section == 0, upper, lower)))
    samples = denoise(
        jnp.concatenate(noise, axis=1),
        jnp.concatenate([condition] * members, axis=1),
        in_ref[...],
        mid_ref[...],
        out_ref[...],
    )
    cells = rows * width
    pieces = [samples[:, m * cells : (m + 1) * cells] for m in range(members)]
    sums_ref[0] = functools.reduce(lambda a, b: a + b, pieces)
    sums_ref[1] = functools.reduce(lambda a, b: a + b, [p * p for p in pieces])


def slot_plan(table, tile, tiles):
    core = lax.rem(tile, 2)
    chip = lax.broadcasted_iota(jnp.int32, table.shape, 0)
    lane = lax.broadcasted_iota(jnp.int32, table.shape, 1)
    device = REACH + core + 2 * lane
    known = chip < 9
    parity = []
    for odd in range(2):
        index = 2 * chip + odd
        ids = tile - core + index - REACH
        ids = jnp.where(ids < 0, ids + tiles, ids)
        ids = jnp.where(ids >= tiles, ids - tiles, ids)
        part = table[:, odd * REACH : (odd + 1) * REACH]
        named = jnp.sum((part >= 0).astype(jnp.float32), axis=1, keepdims=True).astype(jnp.int32)
        begin = table[:, odd * REACH : odd * REACH + 1].astype(jnp.int32) - ids
        begin = jnp.where(begin < 0, begin + tiles, begin)
        behind = device - index
        hit = known & (behind >= begin) & (behind < begin + named)
        parity.append((index, ids, named, hit))
    plans = []
    for row in (REACH + core, REACH + 1 - core):
        target = tile - core + row - REACH
        live, rank, extra = 0, 0, 0
        for index, ids, named, hit in parity:
            live += (hit & (index == row)).astype(jnp.int32)
            rank += (hit & (ids < target)).astype(jnp.int32)
            extra += jnp.where((index == row) & (lane == 0), named, 0)
        live = jnp.sum(live.astype(jnp.float32), axis=0, keepdims=True)
        rank = jnp.sum(rank.astype(jnp.float32), axis=0, keepdims=True)
        weight = jnp.zeros((1, table.shape[1]), jnp.float32)
        for step in range(5):
            weight = jnp.where(lane[:1] == step, float(8**step), weight)
        packed = jnp.sum(weight * live * (rank + 1.0))
        plans.append((packed.astype(jnp.int32), jnp.sum(extra.astype(jnp.float32))))
    return plans


def slot_kernel(*refs, members, ring):
    if ring:
        behind_ref = None
    else:
        behind_ref, *refs = refs
    (
        near_ref,
        far2_ref,
        far4_ref,
        far6_ref,
        far8_ref,
        mine_ref,
        theirs_ref,
        base_ref,
        in_ref,
        mid_ref,
        out_ref,
        own_ref,
        peer_ref,
        noise_ref,
        sample_ref,
        where_ref,
    ) = refs
    records = (near_ref, far2_ref, far4_ref, far6_ref, far8_ref)
    blocks = [record[record.shape[0] - 1].astype(jnp.float32) for record in records]
    ahead = [block[0:1] for block in blocks]
    if ring:
        behind = [ahead[4]] + [block[1:2] for block in blocks[1:4]]
    else:
        behind = [behind_ref[0:4].astype(jnp.float32)]
    spare = jnp.full((7, near_ref.shape[2]), -1.0, jnp.float32)
    table = jnp.concatenate(behind + ahead + [spare], axis=0)
    plans = slot_plan(table, lax.axis_index("tile"), lax.axis_size("tile"))
    channels, cells = mine_ref.shape
    rows, width = noise_ref.shape[2:]
    count = jnp.int32(0)
    for side, (packed, _) in enumerate(plans):
        for step, record in enumerate(records):
            digit = lax.shift_right_logical(packed, 3 * step) & 7
            place = count

            @pl.when(digit > 0)
            def _():
                noise_ref[place] = record[pl.ds(channels * (digit - 1), channels)]
                where_ref[place] = side

            count = count + (digit > 0).astype(jnp.int32)

    own_scale, peer_scale = [1.0 / (members + extra) for _, extra in plans]
    sample_ref[0] = base_ref[...]
    sample_ref[1] = jnp.zeros_like(base_ref)
    w_in, w_mid, w_out = in_ref[...], mid_ref[...], out_ref[...]

    def run(first, group):
        noise, conditions, sides = [], [], []
        for member in range(group):
            side = where_ref[first + member]
            sides.append(side)
            noise.append(flat(noise_ref[first + member]))
            conditions.append(jnp.where(side == 0, mine_ref[...], theirs_ref[...]))
        samples = denoise(
            jnp.concatenate(noise, axis=1), jnp.concatenate(conditions, axis=1), w_in, w_mid, w_out
        )
        for member in range(group):
            sample = samples[:, member * cells : (member + 1) * cells]
            sample_ref[sides[member], 0] += sample
            sample_ref[sides[member], 1] += sample * sample

    fours = count // 4
    left = count - 4 * fours

    @pl.loop(0, fours)
    def _(turn):
        run(4 * turn, 4)

    @pl.when(left >= 2)
    def _():
        run(4 * fours, 2)

    @pl.when((left & 1) == 1)
    def _():
        run(count - 1, 1)

    for moment in range(2):
        own_ref[moment] = (own_scale * sample_ref[0, moment]).reshape(channels, rows, width)
        peer_ref[moment] = (peer_scale * sample_ref[1, moment]).reshape(channels, rows, width)


def in_vmem(count):
    return [pl.BlockSpec(memory_space=pltpu.VMEM)] * count


def from_ahead(block, distance):
    count = lax.axis_size("tile")
    return lax.ppermute(block, "tile", [((i + distance) % count, i) for i in range(count)])


def swap_cores(block):
    count = lax.axis_size("tile")
    return lax.ppermute(block, "tile", [(i, i ^ 1) for i in range(count)])


def swap_sections(block):
    return lax.ppermute(block, "section", [(0, 1), (1, 0)])


def send_edges(rows):
    count = lax.axis_size("tile")
    pairs = [(t, t + 1) for t in range(count - 1)]
    pairs += [(count + t + 1, count + t) for t in range(count - 1)]
    return lax.ppermute(rows, ("section", "tile"), pairs)


def body(
    coarse,
    lift_weight,
    conv_weight,
    out_weight,
    denoise_in,
    denoise_mid,
    denoise_out,
    base_noise,
    slot_noise,
    extra_dest,
):
    section = lax.axis_index("section")
    tile = lax.axis_index("tile")
    count = lax.axis_size("tile")
    slots, channels, rows_all, width = slot_noise.shape
    members = base_noise.shape[0]
    rows = rows_all // SECTIONS
    cells = rows * width
    hidden = denoise_mid.shape[0]
    step_flops = 2 * NSTEP * hidden * (hidden + 3 * channels)
    params = pltpu.CompilerParams(vmem_limit_bytes=VMEM_LIMIT)

    far8_routes = from_ahead(extra_dest, 8)
    edge = jnp.where(section == 0, coarse[:, -1:], coarse[:, :1])
    edge, extra_dest, conv_weight, ends = lax.optimization_barrier(
        (edge, extra_dest, conv_weight, (out_weight, denoise_out))
    )
    edge = send_edges(edge)
    half_conv, half_ends = halved(conv_weight), halved(jnp.concatenate(ends, axis=0))
    routes = jnp.concatenate([extra_dest, far8_routes], axis=0)
    peer_routes = swap_cores(routes)
    even = jnp.where(tile % 2 == 0, routes, peer_routes)
    odd = jnp.where(tile % 2 == 0, peer_routes, routes)
    chip_routes = jnp.concatenate([even, odd], axis=1)
    half_noise = lax.dynamic_slice_in_dim(slot_noise, rows * section, rows, axis=2)
    half_noise = half_noise.reshape(slots * channels, rows, width)
    block = jnp.pad(chip_routes.astype(jnp.bfloat16), ((0, rows - 2), (0, width - 2 * REACH)))
    record = jnp.concatenate([half_noise, block[None]], axis=0)
    far8, far6, far4, far2 = [from_ahead(record, distance) for distance in (8, 6, 4, 2)]

    weight = jax.ShapeDtypeStruct((2 * channels, hidden), jnp.bfloat16)
    condition, w_in, w_mid, w_out = pl.pallas_call(
        regress_kernel,
        out_shape=(
            jax.ShapeDtypeStruct((channels, cells), jnp.bfloat16),
            weight,
            jax.ShapeDtypeStruct(denoise_mid.shape, jnp.bfloat16),
            jax.ShapeDtypeStruct(denoise_out.shape, jnp.bfloat16),
        ),
        in_specs=in_vmem(2) + [pl.BlockSpec(memory_space=pl.ANY)] + in_vmem(2) + [pl.BlockSpec(memory_space=pl.ANY)] * 2,
        out_specs=(pl.BlockSpec(memory_space=pltpu.VMEM),) * 4,
        scratch_shapes=[
            pltpu.VMEM((coarse.shape[0], hidden), jnp.bfloat16),
            pltpu.SemaphoreType.DMA((3,)),
        ],
        compiler_params=params,
        cost_estimate=pl.CostEstimate(
            flops=2 * cells * hidden * (9 * hidden + 16),
            bytes_accessed=600_000,
            transcendentals=2 * cells * hidden,
        ),
        name="regression",
    )(coarse, edge, lift_weight.T, half_conv, half_ends, denoise_in.T, denoise_mid)

    peer_condition = swap_cores(condition)
    ring = count == 2 * REACH
    behind = []
    if not ring:
        block = [from_ahead(chip_routes[:1], -distance) for distance in (8, 6, 4, 2)]
        block = jnp.concatenate(block, axis=0).astype(jnp.bfloat16)
        behind = [jnp.pad(block, ((0, rows - 4), (0, width - 2 * REACH)))]

    base = pl.pallas_call(
        base_kernel,
        out_shape=jax.ShapeDtypeStruct((2, channels, cells), jnp.float32),
        in_specs=in_vmem(5),
        out_specs=pl.BlockSpec(memory_space=pltpu.VMEM),
        compiler_params=params,
        cost_estimate=pl.CostEstimate(
            flops=members * cells * step_flops,
            bytes_accessed=400_000,
            transcendentals=2 * NSTEP * members * cells * hidden,
        ),
        name="base_members",
    )(base_noise, condition, w_in, w_mid, w_out)

    moments = jax.ShapeDtypeStruct((2, channels, rows, width), jnp.float32)
    own, peer = pl.pallas_call(
        functools.partial(slot_kernel, members=members, ring=ring),
        out_shape=(moments, moments),
        in_specs=in_vmem(11 + len(behind)),
        out_specs=(pl.BlockSpec(memory_space=pltpu.VMEM),) * 2,
        scratch_shapes=[
            pltpu.VMEM((12, channels, rows, width), jnp.bfloat16),
            pltpu.VMEM((2, 2, channels, cells), jnp.float32),
            pltpu.SMEM((12,), jnp.int32),
        ],
        compiler_params=params,
        cost_estimate=pl.CostEstimate(
            flops=slots * cells * step_flops,
            bytes_accessed=1_000_000,
            transcendentals=2 * NSTEP * slots * cells * hidden,
        ),
        name="slot_members",
    )(
        *behind,
        record,
        far2,
        far4,
        far6,
        far8,
        condition,
        peer_condition,
        base,
        w_in,
        w_mid,
        w_out,
    )
    total = own + swap_cores(peer)
    mean = total[0]
    variance = total[1] - mean * mean
    kept = jnp.where(section == 0, mean, variance)
    sent = jnp.where(section == 0, variance, mean)
    received = swap_sections(sent)
    upper = jnp.where(section == 0, kept, received)
    lower = jnp.where(section == 0, received, kept)
    return jnp.concatenate([upper, lower], axis=1)[None]


def solution(mesh):
    in_specs = (
        P(None, "tile", None),
        P(),
        P(),
        P(),
        P(),
        P(),
        P(),
        P(None, None, "tile", None),
        P(None, None, "tile", None),
        P("tile", None),
    )
    out_specs = P("section", None, "tile", None)
    return jax.shard_map(body, mesh=mesh, in_specs=in_specs, out_specs=out_specs, check_vma=False)
```

```python
import functools
import math

import jax
import jax.numpy as jnp
from jax import lax
from jax.experimental import pallas as pl
from jax.experimental.pallas import tpu as pltpu
from jax.sharding import PartitionSpec as P

NSTEP = 6
SIGMA_MAX = 4.0
SIGMA_MIN = 0.25
PLAN_POWER = 7.0
SECTIONS = 2
REACH = 8
VMEM_LIMIT = 40 * 1024 * 1024


def sigma_table(step_count):
    upper_root = SIGMA_MAX ** (1.0 / PLAN_POWER)
    lower_root = SIGMA_MIN ** (1.0 / PLAN_POWER)
    values = []
    for position in range(step_count):
        fraction = position / (step_count - 1)
        values.append((upper_root + fraction * (lower_root - upper_root)) ** PLAN_POWER)
    values.append(0.0)
    return values


def step_table():
    sigmas = sigma_table(NSTEP)
    steps = []
    for now, after in zip(sigmas[:-1], sigmas[1:]):
        scale = 1.0 / math.sqrt(now * now + 1.0)
        skip = 1.0 / (now * now + 1.0)
        rate = (after - now) / now
        steps.append((scale, 1.0 + rate * (1.0 - skip), -rate * now * scale))
    return sigmas[0], steps


def half_silu(half):
    return (half * jnp.tanh(half) + half).astype(jnp.bfloat16)


def dot(left, right):
    return jnp.dot(left, right, preferred_element_type=jnp.float32)


def halved(weight):
    return (0.5 * weight.astype(jnp.float32)).astype(jnp.bfloat16)


def dot_rows(left, right):
    return lax.dot_general(
        left, right, (((0,), (0,)), ((), ())), preferred_element_type=jnp.float32
    )


def denoise(noise, condition, w_in, w_mid, w_out):
    start, steps = step_table()
    latent = start * noise
    for scale, keep, gain in steps:
        stacked = jnp.concatenate([(scale * latent).astype(jnp.bfloat16), condition], axis=0)
        hidden = half_silu(dot_rows(w_in, stacked))
        hidden = half_silu(dot(w_mid, hidden))
        latent = keep * latent + gain * dot(w_out, hidden)
    return condition.astype(jnp.float32) + latent


def flat(field):
    return field.astype(jnp.float32).reshape(field.shape[0], -1)


def regress_kernel(
    coarse_ref,
    edge_ref,
    lift_hbm,
    conv_hbm,
    out_hbm,
    in_hbm,
    mid_hbm,
    last_hbm,
    condition_ref,
    in_ref,
    mid_ref,
    last_ref,
    lift_ref,
    conv_ref,
    out_ref,
    sems,
):
    section = lax.axis_index("section")
    channels_in, rows_all, width = coarse_ref.shape
    rows = rows_all // SECTIONS
    pairs = (
        (lift_hbm, lift_ref),
        (conv_hbm, conv_ref),
        (out_hbm, out_ref),
        (in_hbm, in_ref),
        (mid_hbm, mid_ref),
        (last_hbm, last_ref),
    )
    copies = [pltpu.make_async_copy(a, b, sems.at[i]) for i, (a, b) in enumerate(pairs)]
    for copy in copies:
        copy.start()
    coarse = coarse_ref[...].astype(jnp.float32)
    edge = edge_ref[...].astype(jnp.float32)
    upper = jnp.concatenate([edge, coarse[:, : rows + 1]], axis=1)
    lower = jnp.concatenate([coarse[:, rows - 1 :], edge], axis=1)
    window = jnp.where(section == 0, upper, lower)
    window = window.reshape(channels_in, (rows + 2) * width).astype(jnp.bfloat16)
    copies[0].wait()
    half = dot_rows(halved(lift_ref[...]), window)
    lifted = half * jnp.tanh(half) + half
    channels = lifted.shape[0]
    column = lax.broadcasted_iota(jnp.int32, (channels, width), 1)
    taps = []
    for row in range(rows + 2):
        piece = lifted[:, row * width : (row + 1) * width]
        left = jnp.where(column == 0, 0.0, pltpu.roll(piece, 1, 1))
        right = jnp.where(column == width - 1, 0.0, pltpu.roll(piece, width - 1, 1))
        taps.append(jnp.concatenate([left, piece, right], axis=0).astype(jnp.bfloat16))
    stacked = jnp.concatenate(taps, axis=1)
    copies[1].wait()
    half = None
    for tap in range(3):
        weight = halved(conv_ref[tap].reshape(3 * channels, channels))
        part = dot_rows(weight, stacked[:, tap * width : (tap + rows) * width])
        half = part if half is None else half + part
    for copy in copies[2:]:
        copy.wait()
    condition_ref[...] = dot(out_ref[...], half_silu(half)).astype(jnp.bfloat16)
    in_ref[...] = halved(in_ref[...])
    mid_ref[...] = halved(mid_ref[...])


def base_kernel(noise_ref, condition_ref, in_ref, mid_ref, out_ref, *refs, begin, end):
    *earlier, sums_ref = refs
    section = lax.axis_index("section")
    channels, rows_all, width = noise_ref.shape[1:]
    rows = rows_all // SECTIONS
    condition = condition_ref[...]
    noise = []
    for member in range(begin, end):
        upper = noise_ref[member, :, :rows]
        lower = noise_ref[member, :, rows:]
        noise.append(flat(jnp.where(section == 0, upper, lower)))
    samples = denoise(
        jnp.concatenate(noise, axis=1),
        jnp.concatenate([condition] * (end - begin), axis=1),
        in_ref[...],
        mid_ref[...],
        out_ref[...],
    )
    cells = rows * width
    pieces = [samples[:, m * cells : (m + 1) * cells] for m in range(end - begin)]
    sums = [sum(pieces[1:], pieces[0]), sum([p * p for p in pieces[1:]], pieces[0] * pieces[0])]
    for moment in range(2):
        sums_ref[moment] = sums[moment] + (earlier[0][moment] if earlier else 0.0)


def slot_plan(table, tile, tiles):
    core = lax.rem(tile, 2)
    chip = lax.broadcasted_iota(jnp.int32, table.shape, 0)
    lane = lax.broadcasted_iota(jnp.int32, table.shape, 1)
    device = REACH + core + 2 * lane
    known = chip < 9
    parity = []
    for odd in range(2):
        index = 2 * chip + odd
        ids = tile - core + index - REACH
        ids = jnp.where(ids < 0, ids + tiles, ids)
        ids = jnp.where(ids >= tiles, ids - tiles, ids)
        part = table[:, odd * REACH : (odd + 1) * REACH]
        named = jnp.sum((part >= 0).astype(jnp.float32), axis=1, keepdims=True).astype(jnp.int32)
        begin = table[:, odd * REACH : odd * REACH + 1].astype(jnp.int32) - ids
        begin = jnp.where(begin < 0, begin + tiles, begin)
        behind = device - index
        hit = known & (behind >= begin) & (behind < begin + named)
        parity.append((index, ids, named, hit))
    plans = []
    for row in (REACH + core, REACH + 1 - core):
        target = tile - core + row - REACH
        live, rank, extra = 0, 0, 0
        for index, ids, named, hit in parity:
            live += (hit & (index == row)).astype(jnp.int32)
            rank += (hit & (ids < target)).astype(jnp.int32)
            extra += jnp.where((index == row) & (lane == 0), named, 0)
        live = jnp.sum(live.astype(jnp.float32), axis=0, keepdims=True)
        rank = jnp.sum(rank.astype(jnp.float32), axis=0, keepdims=True)
        weight = jnp.zeros((1, table.shape[1]), jnp.float32)
        for step in range(5):
            weight = jnp.where(lane[:1] == step, float(8**step), weight)
        packed = jnp.sum(weight * live * (rank + 1.0))
        plans.append((packed.astype(jnp.int32), jnp.sum(extra.astype(jnp.float32))))
    return plans


def slot_kernel(*refs, members, ring):
    if ring:
        behind_ref = None
    else:
        behind_ref, *refs = refs
    (
        near_ref,
        first_ref,
        second_ref,
        others_ref,
        mine_ref,
        theirs_ref,
        base_ref,
        in_ref,
        mid_ref,
        out_ref,
        own_ref,
        peer_ref,
        noise_ref,
        sample_ref,
        where_ref,
    ) = refs
    section = lax.axis_index("section")
    channels, cells = mine_ref.shape
    rows, width = noise_ref.shape[2:]
    upper, lower = slice(0, rows), slice(rows, SECTIONS * rows)

    def record(step, blocks):
        if step == 0:
            return near_ref[blocks]
        at = (step - 1) // 2
        fetched_ref = (first_ref, second_ref)[at]
        if step % 2 == 1:
            return jnp.where(section == 0, fetched_ref[blocks, upper], others_ref[at, blocks])
        return jnp.where(section == 0, others_ref[at, blocks], fetched_ref[blocks, lower])

    last = near_ref.shape[0] - 1
    blocks = [record(step, slice(last, last + 1))[0].astype(jnp.float32) for step in range(5)]
    ahead = [block[0:1] for block in blocks]
    if ring:
        behind = [ahead[4]] + [block[1:2] for block in blocks[1:4]]
    else:
        behind = [behind_ref[0:4].astype(jnp.float32)]
    spare = jnp.full((7, near_ref.shape[2]), -1.0, jnp.float32)
    table = jnp.concatenate(behind + ahead + [spare], axis=0)
    plans = slot_plan(table, lax.axis_index("tile"), lax.axis_size("tile"))
    count = jnp.int32(0)
    for side, (packed, _) in enumerate(plans):
        for step in range(5):
            digit = lax.shift_right_logical(packed, 3 * step) & 7
            place = count

            @pl.when(digit > 0)
            def _():
                noise_ref[place] = record(step, pl.ds(channels * (digit - 1), channels))
                where_ref[place] = side

            count = count + (digit > 0).astype(jnp.int32)

    own_scale, peer_scale = [1.0 / (members + extra) for _, extra in plans]
    sample_ref[0] = base_ref[...]
    sample_ref[1] = jnp.zeros_like(base_ref)
    w_in, w_mid, w_out = in_ref[...], mid_ref[...], out_ref[...]

    def run(first, group):
        noise, conditions, sides = [], [], []
        for member in range(group):
            side = where_ref[first + member]
            sides.append(side)
            noise.append(flat(noise_ref[first + member]))
            conditions.append(jnp.where(side == 0, mine_ref[...], theirs_ref[...]))
        samples = denoise(
            jnp.concatenate(noise, axis=1), jnp.concatenate(conditions, axis=1), w_in, w_mid, w_out
        )
        for member in range(group):
            sample = samples[:, member * cells : (member + 1) * cells]
            sample_ref[sides[member], 0] += sample
            sample_ref[sides[member], 1] += sample * sample

    fours = count // 4
    left = count - 4 * fours

    @pl.loop(0, fours)
    def _(turn):
        run(4 * turn, 4)

    @pl.when(left >= 2)
    def _():
        run(4 * fours, 2)

    @pl.when((left & 1) == 1)
    def _():
        run(count - 1, 1)

    for moment in range(2):
        own_ref[moment] = (own_scale * sample_ref[0, moment]).reshape(channels, rows, width)
        peer_ref[moment] = (peer_scale * sample_ref[1, moment]).reshape(channels, rows, width)


def in_vmem(count):
    return [pl.BlockSpec(memory_space=pltpu.VMEM)] * count


def from_ahead(block, distance):
    count = lax.axis_size("tile")
    return lax.ppermute(block, "tile", [((i + distance) % count, i) for i in range(count)])


def from_ahead_by(block, distances):
    count = lax.axis_size("tile")
    pairs = []
    for section, distance in enumerate(distances):
        start = section * count
        pairs += [(start + (i + distance) % count, start + i) for i in range(count)]
    return lax.ppermute(block, ("section", "tile"), pairs)


def swap_cores(block):
    count = lax.axis_size("tile")
    return lax.ppermute(block, "tile", [(i, i ^ 1) for i in range(count)])


def swap_sections(block):
    return lax.ppermute(block, "section", [(0, 1), (1, 0)])


def send_edges(rows):
    count = lax.axis_size("tile")
    pairs = [(t, t + 1) for t in range(count - 1)]
    pairs += [(count + t + 1, count + t) for t in range(count - 1)]
    return lax.ppermute(rows, ("section", "tile"), pairs)


def body(
    coarse,
    lift_weight,
    conv_weight,
    out_weight,
    denoise_in,
    denoise_mid,
    denoise_out,
    base_noise,
    slot_noise,
    extra_dest,
):
    section = lax.axis_index("section")
    tile = lax.axis_index("tile")
    count = lax.axis_size("tile")
    slots, channels, rows_all, width = slot_noise.shape
    members = base_noise.shape[0]
    rows = rows_all // SECTIONS
    cells = rows * width
    hidden = denoise_mid.shape[0]
    step_flops = 2 * NSTEP * hidden * (hidden + 3 * channels)
    params = pltpu.CompilerParams(vmem_limit_bytes=VMEM_LIMIT)

    far8_routes = from_ahead(extra_dest, 8)
    edge = jnp.where(section == 0, coarse[:, -1:], coarse[:, :1])
    edge, extra_dest = lax.optimization_barrier((edge, extra_dest))
    edge = send_edges(edge)
    routes = jnp.concatenate([extra_dest, far8_routes], axis=0)
    peer_routes = jnp.concatenate([swap_cores(extra_dest), swap_cores(far8_routes)], axis=0)
    even = jnp.where(tile % 2 == 0, routes, peer_routes)
    odd = jnp.where(tile % 2 == 0, peer_routes, routes)
    chip_routes = jnp.concatenate([even, odd], axis=1)
    block = jnp.pad(chip_routes.astype(jnp.bfloat16), ((0, rows - 2), (0, width - 2 * REACH)))
    block = jnp.concatenate([block, block], axis=0)
    noise = slot_noise.reshape(slots * channels, rows_all, width)
    record = jnp.concatenate([noise, block[None]], axis=0)
    near = lax.dynamic_slice_in_dim(record, rows * section, rows, axis=1)
    first = from_ahead_by(record, (2, 4))
    second = from_ahead_by(record, (6, 8))

    weight = jax.ShapeDtypeStruct((2 * channels, hidden), jnp.bfloat16)
    condition, w_in, w_mid, w_out = pl.pallas_call(
        regress_kernel,
        out_shape=(
            jax.ShapeDtypeStruct((channels, cells), jnp.bfloat16),
            weight,
            jax.ShapeDtypeStruct(denoise_mid.shape, jnp.bfloat16),
            jax.ShapeDtypeStruct(denoise_out.shape, jnp.bfloat16),
        ),
        in_specs=in_vmem(2) + [pl.BlockSpec(memory_space=pltpu.HBM)] * 6,
        out_specs=(pl.BlockSpec(memory_space=pltpu.VMEM),) * 4,
        scratch_shapes=[
            pltpu.VMEM((coarse.shape[0], hidden), jnp.bfloat16),
            pltpu.VMEM(conv_weight.shape, jnp.bfloat16),
            pltpu.VMEM(out_weight.shape, jnp.bfloat16),
            pltpu.SemaphoreType.DMA((6,)),
        ],
        compiler_params=params,
        cost_estimate=pl.CostEstimate(
            flops=2 * cells * hidden * (9 * hidden + 16),
            bytes_accessed=600_000,
            transcendentals=2 * cells * hidden,
        ),
        name="regression",
    )(coarse, edge, lift_weight.T, conv_weight, out_weight, denoise_in.T, denoise_mid, denoise_out)

    peer_condition = swap_cores(condition)
    ring = count == 2 * REACH
    behind = []
    if not ring:
        block = [from_ahead(chip_routes[:1], -distance) for distance in (8, 6, 4, 2)]
        block = jnp.concatenate(block, axis=0).astype(jnp.bfloat16)
        behind = [jnp.pad(block, ((0, rows - 4), (0, width - 2 * REACH)))]

    def base_members(begin, end, *earlier):
        return pl.pallas_call(
            functools.partial(base_kernel, begin=begin, end=end),
            out_shape=jax.ShapeDtypeStruct((2, channels, cells), jnp.float32),
            in_specs=in_vmem(5 + len(earlier)),
            out_specs=pl.BlockSpec(memory_space=pltpu.VMEM),
            compiler_params=params,
            cost_estimate=pl.CostEstimate(
                flops=(end - begin) * cells * step_flops,
                bytes_accessed=400_000,
                transcendentals=2 * NSTEP * (end - begin) * cells * hidden,
            ),
            name="base_members",
        )(base_noise, condition, w_in, w_mid, w_out, *earlier)

    base = base_members(0, members // 2)
    first, second, base = lax.optimization_barrier((first, second, base))
    fetched = jnp.stack([first, second])
    others = jnp.where(section == 0, fetched[:, :, rows:], fetched[:, :, :rows])
    others, base = lax.optimization_barrier((others, base))
    others = swap_sections(others)
    base = base_members(members // 2, members, base)

    moments = jax.ShapeDtypeStruct((2, channels, rows, width), jnp.float32)
    own, peer = pl.pallas_call(
        functools.partial(slot_kernel, members=members, ring=ring),
        out_shape=(moments, moments),
        in_specs=in_vmem(10 + len(behind)),
        out_specs=(pl.BlockSpec(memory_space=pltpu.VMEM),) * 2,
        scratch_shapes=[
            pltpu.VMEM((12, channels, rows, width), jnp.bfloat16),
            pltpu.VMEM((2, 2, channels, cells), jnp.float32),
            pltpu.SMEM((12,), jnp.int32),
        ],
        compiler_params=params,
        cost_estimate=pl.CostEstimate(
            flops=slots * cells * step_flops,
            bytes_accessed=1_000_000,
            transcendentals=2 * NSTEP * slots * cells * hidden,
        ),
        name="slot_members",
    )(
        *behind,
        near,
        first,
        second,
        others,
        condition,
        peer_condition,
        base,
        w_in,
        w_mid,
        w_out,
    )
    total = own + swap_cores(peer)
    mean = total[0]
    variance = total[1] - mean * mean
    kept = jnp.where(section == 0, mean, variance)
    sent = jnp.where(section == 0, variance, mean)
    received = swap_sections(sent)
    upper = jnp.where(section == 0, kept, received)
    lower = jnp.where(section == 0, received, kept)
    return jnp.concatenate([upper, lower], axis=1)[None]


def solution(mesh):
    in_specs = (
        P(None, "tile", None),
        P(),
        P(),
        P(),
        P(),
        P(),
        P(),
        P(None, None, "tile", None),
        P(None, None, "tile", None),
        P("tile", None),
    )
    out_specs = P("section", None, "tile", None)
    return jax.shard_map(body, mesh=mesh, in_specs=in_specs, out_specs=out_specs, check_vma=False)
```

```python
import functools
import math

import jax
import jax.numpy as jnp
from jax import lax
from jax.experimental import pallas as pl
from jax.experimental.pallas import tpu as pltpu
from jax.sharding import PartitionSpec as P

NSTEP = 6
SIGMA_MAX = 4.0
SIGMA_MIN = 0.25
PLAN_POWER = 7.0
SECTIONS = 2
REACH = 8
PLANE = 4
VMEM_LIMIT = 40 * 1024 * 1024


def sigma_table(step_count):
    upper_root = SIGMA_MAX ** (1.0 / PLAN_POWER)
    lower_root = SIGMA_MIN ** (1.0 / PLAN_POWER)
    values = []
    for position in range(step_count):
        fraction = position / (step_count - 1)
        values.append((upper_root + fraction * (lower_root - upper_root)) ** PLAN_POWER)
    values.append(0.0)
    return values


def step_table():
    sigmas = sigma_table(NSTEP)
    steps = []
    for now, after in zip(sigmas[:-1], sigmas[1:]):
        scale = 1.0 / math.sqrt(now * now + 1.0)
        skip = 1.0 / (now * now + 1.0)
        rate = (after - now) / now
        steps.append((scale, 1.0 + rate * (1.0 - skip), -rate * now * scale))
    return sigmas[0], steps


def half_silu(half):
    return (half * jnp.tanh(half) + half).astype(jnp.bfloat16)


def dot(left, right):
    return jnp.dot(left, right, preferred_element_type=jnp.float32)


def halved(weight):
    return (0.5 * weight.astype(jnp.float32)).astype(jnp.bfloat16)


def dot_rows(left, right):
    return lax.dot_general(
        left, right, (((0,), (0,)), ((), ())), preferred_element_type=jnp.float32
    )


def denoise(noise, condition, w_in, w_mid, w_out):
    start, steps = step_table()
    latent = start * noise
    for scale, keep, gain in steps:
        stacked = jnp.concatenate([(scale * latent).astype(jnp.bfloat16), condition], axis=0)
        hidden = half_silu(dot_rows(w_in, stacked))
        hidden = half_silu(dot(w_mid, hidden))
        latent = keep * latent + gain * dot(w_out, hidden)
    return condition.astype(jnp.float32) + latent


def flat(field):
    return field.astype(jnp.float32).reshape(field.shape[0], -1)


def regress_kernel(coarse_ref, edge_ref, lift_ref, conv_ref, out_ref, condition_ref):
    section = lax.axis_index("section")
    channels_in, rows_all, width = coarse_ref.shape
    rows = rows_all // SECTIONS
    coarse = coarse_ref[...].astype(jnp.float32)
    edge = edge_ref[...].astype(jnp.float32)
    upper = jnp.concatenate([edge, coarse[:, : rows + 1]], axis=1)
    lower = jnp.concatenate([coarse[:, rows - 1 :], edge], axis=1)
    window = jnp.where(section == 0, upper, lower)
    window = window.reshape(channels_in, (rows + 2) * width).astype(jnp.bfloat16)
    half = dot_rows(halved(lift_ref[...]), window)
    lifted = half * jnp.tanh(half) + half
    channels = lifted.shape[0]
    column = lax.broadcasted_iota(jnp.int32, (channels, width), 1)
    taps = []
    for row in range(rows + 2):
        piece = lifted[:, row * width : (row + 1) * width]
        left = jnp.where(column == 0, 0.0, pltpu.roll(piece, 1, 1))
        right = jnp.where(column == width - 1, 0.0, pltpu.roll(piece, width - 1, 1))
        taps.append(jnp.concatenate([left, piece, right], axis=0).astype(jnp.bfloat16))
    stacked = jnp.concatenate(taps, axis=1)
    half = None
    for tap in range(3):
        weight = halved(conv_ref[tap].reshape(3 * channels, channels))
        part = dot_rows(weight, stacked[:, tap * width : (tap + rows) * width])
        half = part if half is None else half + part
    condition_ref[...] = dot(out_ref[...], half_silu(half)).astype(jnp.bfloat16)


def base_kernel(noise_ref, condition_ref, in_ref, mid_ref, out_ref, sums_ref):
    section = lax.axis_index("section")
    members, channels, rows_all, width = noise_ref.shape
    rows = rows_all // SECTIONS
    condition = condition_ref[...]
    noise = []
    for member in range(members):
        upper = noise_ref[member, :, :rows]
        lower = noise_ref[member, :, rows:]
        noise.append(flat(jnp.where(section == 0, upper, lower)))
    samples = denoise(
        jnp.concatenate(noise, axis=1),
        jnp.concatenate([condition] * members, axis=1),
        halved(in_ref[...]),
        halved(mid_ref[...]),
        out_ref[...],
    )
    cells = rows * width
    pieces = [samples[:, m * cells : (m + 1) * cells] for m in range(members)]
    sums_ref[0] = functools.reduce(lambda a, b: a + b, pieces)
    sums_ref[1] = functools.reduce(lambda a, b: a + b, [p * p for p in pieces])


def slot_plan(table, tile, tiles, slots, ring):
    place = lax.rem(tile, PLANE)
    first = tile - place
    other = place + 1 - 2 * lax.rem(tile, 2)
    chip = lax.broadcasted_iota(jnp.int32, table.shape, 0)
    lane = lax.broadcasted_iota(jnp.int32, table.shape, 1)
    device = REACH + place + 2 * lane
    parity = []
    for odd in range(2):
        index = 2 * chip + odd
        ids = first + index - REACH
        ids = jnp.where(ids < 0, ids + tiles, ids)
        ids = jnp.where(ids >= tiles, ids - tiles, ids)
        part = table[:, odd * REACH : (odd + 1) * REACH]
        named = jnp.sum((part >= 0).astype(jnp.float32), axis=1, keepdims=True).astype(jnp.int32)
        begin = table[:, odd * REACH : odd * REACH + 1].astype(jnp.int32) - ids
        begin = jnp.where(begin < 0, begin + tiles, begin)
        behind = device - index
        hit = (behind >= begin) & (behind < begin + named)
        parity.append((index, ids, named, hit))
    plans = []
    for at in (place, other):
        target = first + at
        live, before, after, extra = 0, 0, 0, 0
        for index, ids, named, hit in parity:
            here = index == REACH + at
            live += (hit & here).astype(jnp.float32)
            before += (hit & (ids < target)).astype(jnp.float32)
            after += (hit & (ids > target)).astype(jnp.float32)
            extra += jnp.where(here & (lane == 0), named, 0).astype(jnp.float32)
        live = jnp.sum(live, axis=0, keepdims=True)
        rank = jnp.sum(before, axis=0, keepdims=True)
        if ring:
            later = jnp.sum(after, axis=0, keepdims=True)
            rank = jnp.where(first == 0, rank, slots - 1.0 - later)
        weight = jnp.zeros((1, table.shape[1]), jnp.float32)
        for step in range(5):
            weight = jnp.where(lane[:1] == step, float(8**step), weight)
        packed = jnp.sum(weight * jnp.where(live > 0, rank + 1.0, 0.0))
        plans.append((packed.astype(jnp.int32), jnp.sum(extra)))
    return plans


def slot_kernel(*refs, members, slots, ring):
    if ring:
        behind_ref = None
    else:
        behind_ref, *refs = refs
    (
        plane_ref,
        plane4_ref,
        plane8_ref,
        mine_ref,
        theirs_ref,
        base_ref,
        in_ref,
        mid_ref,
        out_ref,
        own_ref,
        peer_ref,
        noise_ref,
        sample_ref,
        where_ref,
    ) = refs
    planes = (plane_ref, plane4_ref, plane8_ref)
    tile = lax.axis_index("tile")
    leading = lax.rem(tile, PLANE) < 2
    channels, cells = mine_ref.shape
    rows, width = noise_ref.shape[2:]
    blocks = plane_ref.shape[0] // 2
    table = []
    for plane in planes:
        same = plane[blocks - 1].astype(jnp.float32)[:1]
        across = plane[2 * blocks - 1].astype(jnp.float32)[:1]
        table += [jnp.where(leading, same, across), jnp.where(leading, across, same)]
    if ring:
        behind = jnp.concatenate(table[4:] + [jnp.full((2, width), -1.0, jnp.float32)], axis=0)
    else:
        behind = behind_ref[0:4].astype(jnp.float32)
    spare = jnp.full((6, width), -1.0, jnp.float32)
    table = jnp.concatenate([behind] + table + [spare], axis=0)
    plans = slot_plan(table, tile, lax.axis_size("tile"), slots, ring)

    def noise_of(step, slot):
        start = channels * slot
        if step % 2 == 0:
            return planes[step // 2][pl.ds(start, channels)]
        start = blocks + start
        near = planes[step // 2][pl.ds(start, channels)]
        far = planes[step // 2 + 1][pl.ds(start, channels)]
        return jnp.where(leading, near, far)

    count = jnp.int32(0)
    for side, (packed, _) in enumerate(plans):
        for step in range(5):
            digit = lax.shift_right_logical(packed, 3 * step) & 7
            place = count

            @pl.when(digit > 0)
            def _():
                noise_ref[place] = noise_of(step, digit - 1)
                where_ref[place] = side

            count = count + (digit > 0).astype(jnp.int32)

    own_scale, peer_scale = [1.0 / (members + extra) for _, extra in plans]
    sample_ref[0] = base_ref[...]
    sample_ref[1] = jnp.zeros_like(base_ref)
    w_in, w_mid, w_out = halved(in_ref[...]), halved(mid_ref[...]), out_ref[...]

    def run(first, group):
        noise, conditions, sides = [], [], []
        for member in range(group):
            side = where_ref[first + member]
            sides.append(side)
            noise.append(flat(noise_ref[first + member]))
            conditions.append(jnp.where(side == 0, mine_ref[...], theirs_ref[...]))
        samples = denoise(
            jnp.concatenate(noise, axis=1), jnp.concatenate(conditions, axis=1), w_in, w_mid, w_out
        )
        for member in range(group):
            sample = samples[:, member * cells : (member + 1) * cells]
            sample_ref[sides[member], 0] += sample
            sample_ref[sides[member], 1] += sample * sample

    fours = count // 4
    left = count - 4 * fours

    @pl.loop(0, fours)
    def _(turn):
        run(4 * turn, 4)

    @pl.when(left >= 2)
    def _():
        run(4 * fours, 2)

    @pl.when((left & 1) == 1)
    def _():
        run(count - 1, 1)

    for moment in range(2):
        own_ref[moment] = (own_scale * sample_ref[0, moment]).reshape(channels, rows, width)
        peer_ref[moment] = (peer_scale * sample_ref[1, moment]).reshape(channels, rows, width)


def in_vmem(count):
    return [pl.BlockSpec(memory_space=pltpu.VMEM)] * count


def from_ahead(block, distance):
    count = lax.axis_size("tile")
    return lax.ppermute(block, "tile", [((i + distance) % count, i) for i in range(count)])


def swap_cores(block):
    count = lax.axis_size("tile")
    return lax.ppermute(block, "tile", [(i, i ^ 1) for i in range(count)])


def swap_chips(block):
    count = lax.axis_size("tile")
    return lax.ppermute(block, "tile", [(i, i ^ 2) for i in range(count)])


def swap_sections(block):
    return lax.ppermute(block, "section", [(0, 1), (1, 0)])


def send_edges(rows):
    count = lax.axis_size("tile")
    pairs = [(t, t + 1) for t in range(count - 1)]
    pairs += [(count + t + 1, count + t) for t in range(count - 1)]
    return lax.ppermute(rows, ("section", "tile"), pairs)


def body(
    coarse,
    lift_weight,
    conv_weight,
    out_weight,
    denoise_in,
    denoise_mid,
    denoise_out,
    base_noise,
    slot_noise,
    extra_dest,
):
    section = lax.axis_index("section")
    tile = lax.axis_index("tile")
    count = lax.axis_size("tile")
    slots, channels, rows_all, width = slot_noise.shape
    members = base_noise.shape[0]
    rows = rows_all // SECTIONS
    cells = rows * width
    hidden = denoise_mid.shape[0]
    step_flops = 2 * NSTEP * hidden * (hidden + 3 * channels)
    params = pltpu.CompilerParams(vmem_limit_bytes=VMEM_LIMIT)

    peer_routes = swap_cores(extra_dest)
    edge = jnp.where(section == 0, coarse[:, -1:], coarse[:, :1])
    edge, extra_dest, conv_weight, peer_routes = lax.optimization_barrier(
        (edge, extra_dest, conv_weight, peer_routes)
    )
    edge = send_edges(edge)
    conv_weight = swap_cores(conv_weight)
    even = jnp.where(tile % 2 == 0, extra_dest, peer_routes)
    odd = jnp.where(tile % 2 == 0, peer_routes, extra_dest)
    chip_routes = jnp.concatenate([even, odd], axis=1)
    half_noise = lax.dynamic_slice_in_dim(slot_noise, rows * section, rows, axis=2)
    half_noise = half_noise.reshape(slots * channels, rows, width)
    block = jnp.pad(chip_routes.astype(jnp.bfloat16), ((0, rows - 1), (0, width - 2 * REACH)))
    record = jnp.concatenate([half_noise, block[None]], axis=0)
    across = swap_chips(record)

    condition = pl.pallas_call(
        regress_kernel,
        out_shape=jax.ShapeDtypeStruct((channels, cells), jnp.bfloat16),
        in_specs=in_vmem(5),
        out_specs=pl.BlockSpec(memory_space=pltpu.VMEM),
        compiler_params=params,
        cost_estimate=pl.CostEstimate(
            flops=2 * cells * hidden * (9 * hidden + 16),
            bytes_accessed=600_000,
            transcendentals=2 * cells * hidden,
        ),
        name="regression",
    )(coarse, edge, lift_weight.T, conv_weight, out_weight)

    across, condition = lax.optimization_barrier((across, condition))
    plane = jnp.concatenate([record, across], axis=0)
    plane4, plane8 = from_ahead(plane, PLANE), from_ahead(plane, 2 * PLANE)
    peer_condition = swap_cores(condition)
    ring = count == 2 * REACH
    behind = []
    if not ring:
        chips = [block[:1, : 2 * REACH], across[-1, :1, : 2 * REACH]]
        leading = tile % PLANE < 2
        chips = [jnp.where(leading, *chips), jnp.where(leading, *chips[::-1])]
        chips = jnp.concatenate(chips, axis=0)
        chips = [from_ahead(chips, -2 * PLANE), from_ahead(chips, -PLANE)]
        chips = jnp.concatenate(chips, axis=0)
        behind = [jnp.pad(chips, ((0, rows - 4), (0, width - 2 * REACH)))]

    base = pl.pallas_call(
        base_kernel,
        out_shape=jax.ShapeDtypeStruct((2, channels, cells), jnp.float32),
        in_specs=in_vmem(5),
        out_specs=pl.BlockSpec(memory_space=pltpu.VMEM),
        compiler_params=params,
        cost_estimate=pl.CostEstimate(
            flops=members * cells * step_flops,
            bytes_accessed=400_000,
            transcendentals=2 * NSTEP * members * cells * hidden,
        ),
        name="base_members",
    )(base_noise, condition, denoise_in.T, denoise_mid, denoise_out)

    moments = jax.ShapeDtypeStruct((2, channels, rows, width), jnp.float32)
    own, peer = pl.pallas_call(
        functools.partial(slot_kernel, members=members, slots=slots, ring=ring),
        out_shape=(moments, moments),
        in_specs=in_vmem(9 + len(behind)),
        out_specs=(pl.BlockSpec(memory_space=pltpu.VMEM),) * 2,
        scratch_shapes=[
            pltpu.VMEM((12, channels, rows, width), jnp.bfloat16),
            pltpu.VMEM((2, 2, channels, cells), jnp.float32),
            pltpu.SMEM((12,), jnp.int32),
        ],
        compiler_params=params,
        cost_estimate=pl.CostEstimate(
            flops=slots * cells * step_flops,
            bytes_accessed=1_000_000,
            transcendentals=2 * NSTEP * slots * cells * hidden,
        ),
        name="slot_members",
    )(
        *behind,
        plane,
        plane4,
        plane8,
        condition,
        peer_condition,
        base,
        denoise_in.T,
        denoise_mid,
        denoise_out,
    )
    total = own + swap_cores(peer)
    mean = total[0]
    variance = total[1] - mean * mean
    kept = jnp.where(section == 0, mean, variance)
    sent = jnp.where(section == 0, variance, mean)
    received = swap_sections(sent)
    upper = jnp.where(section == 0, kept, received)
    lower = jnp.where(section == 0, received, kept)
    return jnp.concatenate([upper, lower], axis=1)[None]


def solution(mesh):
    in_specs = (
        P(None, "tile", None),
        P(),
        P(),
        P(),
        P(),
        P(),
        P(),
        P(None, None, "tile", None),
        P(None, None, "tile", None),
        P("tile", None),
    )
    out_specs = P("section", None, "tile", None)
    return jax.shard_map(body, mesh=mesh, in_specs=in_specs, out_specs=out_specs, check_vma=False)
```

```python
import functools
import math

import jax
import jax.numpy as jnp
from jax import lax
from jax.experimental import pallas as pl
from jax.experimental.pallas import tpu as pltpu
from jax.sharding import PartitionSpec as P

NSTEP = 6
SIGMA_MAX = 4.0
SIGMA_MIN = 0.25
PLAN_POWER = 7.0
SECTIONS = 2
REACH = 8
PLANE = 4
VMEM_LIMIT = 40 * 1024 * 1024


def sigma_table(step_count):
    upper_root = SIGMA_MAX ** (1.0 / PLAN_POWER)
    lower_root = SIGMA_MIN ** (1.0 / PLAN_POWER)
    values = []
    for position in range(step_count):
        fraction = position / (step_count - 1)
        values.append((upper_root + fraction * (lower_root - upper_root)) ** PLAN_POWER)
    values.append(0.0)
    return values


def step_table():
    sigmas = sigma_table(NSTEP)
    steps = []
    for now, after in zip(sigmas[:-1], sigmas[1:]):
        scale = 1.0 / math.sqrt(now * now + 1.0)
        skip = 1.0 / (now * now + 1.0)
        rate = (after - now) / now
        steps.append((scale, 1.0 + rate * (1.0 - skip), -rate * now * scale))
    return sigmas[0], steps


def half_silu(half):
    return (half * jnp.tanh(half) + half).astype(jnp.bfloat16)


def dot(left, right):
    return jnp.dot(left, right, preferred_element_type=jnp.float32)


def halved(weight):
    return (0.5 * weight.astype(jnp.float32)).astype(jnp.bfloat16)


def dot_rows(left, right):
    return lax.dot_general(
        left, right, (((0,), (0,)), ((), ())), preferred_element_type=jnp.float32
    )


def denoise(noise, condition, w_in, w_mid, w_out):
    start, steps = step_table()
    latent = start * noise
    for scale, keep, gain in steps:
        stacked = jnp.concatenate([(scale * latent).astype(jnp.bfloat16), condition], axis=0)
        hidden = half_silu(dot_rows(w_in, stacked))
        hidden = half_silu(dot(w_mid, hidden))
        latent = keep * latent + gain * dot(w_out, hidden)
    return condition.astype(jnp.float32) + latent


def flat(field):
    return field.astype(jnp.float32).reshape(field.shape[0], -1)


def regress_kernel(coarse_ref, edge_ref, lift_ref, conv_ref, out_ref, condition_ref):
    section = lax.axis_index("section")
    channels_in, rows_all, width = coarse_ref.shape
    rows = rows_all // SECTIONS
    coarse = coarse_ref[...].astype(jnp.float32)
    edge = edge_ref[...].astype(jnp.float32)
    upper = jnp.concatenate([edge, coarse[:, : rows + 1]], axis=1)
    lower = jnp.concatenate([coarse[:, rows - 1 :], edge], axis=1)
    window = jnp.where(section == 0, upper, lower)
    window = window.reshape(channels_in, (rows + 2) * width).astype(jnp.bfloat16)
    half = dot_rows(halved(lift_ref[...]), window)
    lifted = half * jnp.tanh(half) + half
    channels = lifted.shape[0]
    column = lax.broadcasted_iota(jnp.int32, (channels, width), 1)
    taps = []
    for row in range(rows + 2):
        piece = lifted[:, row * width : (row + 1) * width]
        left = jnp.where(column == 0, 0.0, pltpu.roll(piece, 1, 1))
        right = jnp.where(column == width - 1, 0.0, pltpu.roll(piece, width - 1, 1))
        taps.append(jnp.concatenate([left, piece, right], axis=0).astype(jnp.bfloat16))
    stacked = jnp.concatenate(taps, axis=1)
    half = None
    for tap in range(3):
        weight = halved(conv_ref[tap].reshape(3 * channels, channels))
        part = dot_rows(weight, stacked[:, tap * width : (tap + rows) * width])
        half = part if half is None else half + part
    condition_ref[...] = dot(out_ref[...], half_silu(half)).astype(jnp.bfloat16)


def base_kernel(noise_ref, condition_ref, in_ref, mid_ref, out_ref, sums_ref):
    section = lax.axis_index("section")
    members, channels, rows_all, width = noise_ref.shape
    rows = rows_all // SECTIONS
    condition = condition_ref[...]
    noise = []
    for member in range(members):
        upper = noise_ref[member, :, :rows]
        lower = noise_ref[member, :, rows:]
        noise.append(flat(jnp.where(section == 0, upper, lower)))
    samples = denoise(
        jnp.concatenate(noise, axis=1),
        jnp.concatenate([condition] * members, axis=1),
        halved(in_ref[...]),
        halved(mid_ref[...]),
        out_ref[...],
    )
    cells = rows * width
    pieces = [samples[:, m * cells : (m + 1) * cells] for m in range(members)]
    sums_ref[0] = functools.reduce(lambda a, b: a + b, pieces)
    sums_ref[1] = functools.reduce(lambda a, b: a + b, [p * p for p in pieces])


def slot_plan(table, tile, tiles, slots, ring):
    place = lax.rem(tile, PLANE)
    first = tile - place
    other = place + 1 - 2 * lax.rem(tile, 2)
    chip = lax.broadcasted_iota(jnp.int32, table.shape, 0)
    lane = lax.broadcasted_iota(jnp.int32, table.shape, 1)
    device = REACH + place + 2 * lane
    parity = []
    for odd in range(2):
        index = 2 * chip + odd
        ids = first + index - REACH
        ids = jnp.where(ids < 0, ids + tiles, ids)
        ids = jnp.where(ids >= tiles, ids - tiles, ids)
        part = table[:, odd * REACH : (odd + 1) * REACH]
        named = jnp.sum((part >= 0).astype(jnp.float32), axis=1, keepdims=True).astype(jnp.int32)
        begin = table[:, odd * REACH : odd * REACH + 1].astype(jnp.int32) - ids
        begin = jnp.where(begin < 0, begin + tiles, begin)
        behind = device - index
        hit = (behind >= begin) & (behind < begin + named)
        parity.append((index, ids, named, hit))
    plans = []
    for at in (place, other):
        target = first + at
        live, before, after, extra = 0, 0, 0, 0
        for index, ids, named, hit in parity:
            here = index == REACH + at
            live += (hit & here).astype(jnp.float32)
            before += (hit & (ids < target)).astype(jnp.float32)
            after += (hit & (ids > target)).astype(jnp.float32)
            extra += jnp.where(here & (lane == 0), named, 0).astype(jnp.float32)
        live = jnp.sum(live, axis=0, keepdims=True)
        rank = jnp.sum(before, axis=0, keepdims=True)
        if ring:
            later = jnp.sum(after, axis=0, keepdims=True)
            rank = jnp.where(first == 0, rank, slots - 1.0 - later)
        weight = jnp.zeros((1, table.shape[1]), jnp.float32)
        for step in range(5):
            weight = jnp.where(lane[:1] == step, float(8**step), weight)
        packed = jnp.sum(weight * jnp.where(live > 0, rank + 1.0, 0.0))
        plans.append((packed.astype(jnp.int32), jnp.sum(extra)))
    return plans


def slot_kernel(*refs, members, slots, ring):
    if ring:
        behind_ref = None
    else:
        behind_ref, *refs = refs
    (
        plane_ref,
        plane4_ref,
        plane8_ref,
        mine_ref,
        theirs_ref,
        base_ref,
        in_ref,
        mid_ref,
        out_ref,
        own_ref,
        peer_ref,
        noise_ref,
        sample_ref,
        where_ref,
    ) = refs
    planes = (plane_ref, plane4_ref, plane8_ref)
    tile = lax.axis_index("tile")
    leading = lax.rem(tile, PLANE) < 2
    channels, cells = mine_ref.shape
    rows, width = noise_ref.shape[2:]
    blocks = plane_ref.shape[0] // 2
    table = []
    for plane in planes:
        same = plane[blocks - 1].astype(jnp.float32)[:1]
        across = plane[2 * blocks - 1].astype(jnp.float32)[:1]
        table += [jnp.where(leading, same, across), jnp.where(leading, across, same)]
    if ring:
        behind = jnp.concatenate(table[4:] + [jnp.full((2, width), -1.0, jnp.float32)], axis=0)
    else:
        behind = behind_ref[0:4].astype(jnp.float32)
    spare = jnp.full((6, width), -1.0, jnp.float32)
    table = jnp.concatenate([behind] + table + [spare], axis=0)
    plans = slot_plan(table, tile, lax.axis_size("tile"), slots, ring)

    def noise_of(step, slot):
        start = channels * slot
        if step % 2 == 0:
            return planes[step // 2][pl.ds(start, channels)]
        start = blocks + start
        near = planes[step // 2][pl.ds(start, channels)]
        far = planes[step // 2 + 1][pl.ds(start, channels)]
        return jnp.where(leading, near, far)

    count = jnp.int32(0)
    for side, (packed, _) in enumerate(plans):
        for step in range(5):
            digit = lax.shift_right_logical(packed, 3 * step) & 7
            place = count

            @pl.when(digit > 0)
            def _():
                noise_ref[place] = noise_of(step, digit - 1)
                where_ref[place] = side

            count = count + (digit > 0).astype(jnp.int32)

    own_scale, peer_scale = [1.0 / (members + extra) for _, extra in plans]
    sample_ref[0] = base_ref[...]
    sample_ref[1] = jnp.zeros_like(base_ref)
    w_in, w_mid, w_out = halved(in_ref[...]), halved(mid_ref[...]), out_ref[...]

    def run(first, group):
        noise, conditions, sides = [], [], []
        for member in range(group):
            side = where_ref[first + member]
            sides.append(side)
            noise.append(flat(noise_ref[first + member]))
            conditions.append(jnp.where(side == 0, mine_ref[...], theirs_ref[...]))
        samples = denoise(
            jnp.concatenate(noise, axis=1), jnp.concatenate(conditions, axis=1), w_in, w_mid, w_out
        )
        for member in range(group):
            sample = samples[:, member * cells : (member + 1) * cells]
            sample_ref[sides[member], 0] += sample
            sample_ref[sides[member], 1] += sample * sample

    fours = count // 4
    left = count - 4 * fours

    @pl.loop(0, fours)
    def _(turn):
        run(4 * turn, 4)

    @pl.when(left >= 2)
    def _():
        run(4 * fours, 2)

    @pl.when((left & 1) == 1)
    def _():
        run(count - 1, 1)

    for moment in range(2):
        own_ref[moment] = (own_scale * sample_ref[0, moment]).reshape(channels, rows, width)
        peer_ref[moment] = (peer_scale * sample_ref[1, moment]).reshape(channels, rows, width)


def in_vmem(count):
    return [pl.BlockSpec(memory_space=pltpu.VMEM)] * count


def from_ahead(block, distance):
    count = lax.axis_size("tile")
    return lax.ppermute(block, "tile", [((i + distance) % count, i) for i in range(count)])


def swap_cores(block):
    count = lax.axis_size("tile")
    return lax.ppermute(block, "tile", [(i, i ^ 1) for i in range(count)])


def swap_chips(block):
    count = lax.axis_size("tile")
    return lax.ppermute(block, "tile", [(i, i ^ 2) for i in range(count)])


def swap_sections(block):
    return lax.ppermute(block, "section", [(0, 1), (1, 0)])


def send_edges(rows):
    count = lax.axis_size("tile")
    pairs = [(t, t + 1) for t in range(count - 1)]
    pairs += [(count + t + 1, count + t) for t in range(count - 1)]
    return lax.ppermute(rows, ("section", "tile"), pairs)


def body(
    coarse,
    lift_weight,
    conv_weight,
    out_weight,
    denoise_in,
    denoise_mid,
    denoise_out,
    base_noise,
    slot_noise,
    extra_dest,
):
    section = lax.axis_index("section")
    tile = lax.axis_index("tile")
    count = lax.axis_size("tile")
    slots, channels, rows_all, width = slot_noise.shape
    members = base_noise.shape[0]
    rows = rows_all // SECTIONS
    cells = rows * width
    hidden = denoise_mid.shape[0]
    step_flops = 2 * NSTEP * hidden * (hidden + 3 * channels)
    params = pltpu.CompilerParams(vmem_limit_bytes=VMEM_LIMIT)

    peer_routes = swap_cores(extra_dest)
    edge = jnp.where(section == 0, coarse[:, -1:], coarse[:, :1])
    edge, extra_dest, conv_weight, denoise_out, peer_routes = lax.optimization_barrier(
        (edge, extra_dest, conv_weight, denoise_out, peer_routes)
    )
    edge = send_edges(edge)
    conv_weight, denoise_out = swap_cores(conv_weight), swap_cores(denoise_out)
    even = jnp.where(tile % 2 == 0, extra_dest, peer_routes)
    odd = jnp.where(tile % 2 == 0, peer_routes, extra_dest)
    chip_routes = jnp.concatenate([even, odd], axis=1)
    half_noise = lax.dynamic_slice_in_dim(slot_noise, rows * section, rows, axis=2)
    half_noise = half_noise.reshape(slots * channels, rows, width)
    block = jnp.pad(chip_routes.astype(jnp.bfloat16), ((0, rows - 1), (0, width - 2 * REACH)))
    record = jnp.concatenate([half_noise, block[None]], axis=0)
    across = swap_chips(record)

    condition = pl.pallas_call(
        regress_kernel,
        out_shape=jax.ShapeDtypeStruct((channels, cells), jnp.bfloat16),
        in_specs=in_vmem(5),
        out_specs=pl.BlockSpec(memory_space=pltpu.VMEM),
        compiler_params=params,
        cost_estimate=pl.CostEstimate(
            flops=2 * cells * hidden * (9 * hidden + 16),
            bytes_accessed=600_000,
            transcendentals=2 * cells * hidden,
        ),
        name="regression",
    )(coarse, edge, lift_weight.T, conv_weight, out_weight)

    plane = jnp.concatenate([record, across], axis=0)
    plane4, plane8 = from_ahead(plane, PLANE), from_ahead(plane, 2 * PLANE)
    peer_condition = swap_cores(condition)
    ring = count == 2 * REACH
    behind = []
    if not ring:
        chips = [block[:1, : 2 * REACH], across[-1, :1, : 2 * REACH]]
        leading = tile % PLANE < 2
        chips = [jnp.where(leading, *chips), jnp.where(leading, *chips[::-1])]
        chips = jnp.concatenate(chips, axis=0)
        chips = [from_ahead(chips, -2 * PLANE), from_ahead(chips, -PLANE)]
        chips = jnp.concatenate(chips, axis=0)
        behind = [jnp.pad(chips, ((0, rows - 4), (0, width - 2 * REACH)))]

    base = pl.pallas_call(
        base_kernel,
        out_shape=jax.ShapeDtypeStruct((2, channels, cells), jnp.float32),
        in_specs=in_vmem(5),
        out_specs=pl.BlockSpec(memory_space=pltpu.VMEM),
        compiler_params=params,
        cost_estimate=pl.CostEstimate(
            flops=members * cells * step_flops,
            bytes_accessed=400_000,
            transcendentals=2 * NSTEP * members * cells * hidden,
        ),
        name="base_members",
    )(base_noise, condition, denoise_in.T, denoise_mid, denoise_out)

    moments = jax.ShapeDtypeStruct((2, channels, rows, width), jnp.float32)
    own, peer = pl.pallas_call(
        functools.partial(slot_kernel, members=members, slots=slots, ring=ring),
        out_shape=(moments, moments),
        in_specs=in_vmem(9 + len(behind)),
        out_specs=(pl.BlockSpec(memory_space=pltpu.VMEM),) * 2,
        scratch_shapes=[
            pltpu.VMEM((12, channels, rows, width), jnp.bfloat16),
            pltpu.VMEM((2, 2, channels, cells), jnp.float32),
            pltpu.SMEM((12,), jnp.int32),
        ],
        compiler_params=params,
        cost_estimate=pl.CostEstimate(
            flops=slots * cells * step_flops,
            bytes_accessed=1_000_000,
            transcendentals=2 * NSTEP * slots * cells * hidden,
        ),
        name="slot_members",
    )(
        *behind,
        plane,
        plane4,
        plane8,
        condition,
        peer_condition,
        base,
        denoise_in.T,
        denoise_mid,
        denoise_out,
    )
    total = own + swap_cores(peer)
    mean = total[0]
    variance = total[1] - mean * mean
    kept = jnp.where(section == 0, mean, variance)
    sent = jnp.where(section == 0, variance, mean)
    received = swap_sections(sent)
    upper = jnp.where(section == 0, kept, received)
    lower = jnp.where(section == 0, received, kept)
    return jnp.concatenate([upper, lower], axis=1)[None]


def solution(mesh):
    in_specs = (
        P(None, "tile", None),
        P(),
        P(),
        P(),
        P(),
        P(),
        P(),
        P(None, None, "tile", None),
        P(None, None, "tile", None),
        P("tile", None),
    )
    out_specs = P("section", None, "tile", None)
    return jax.shard_map(body, mesh=mesh, in_specs=in_specs, out_specs=out_specs, check_vma=False)
```

```python
import functools
import math

import jax
import jax.numpy as jnp
from jax import lax
from jax.experimental import pallas as pl
from jax.experimental.pallas import tpu as pltpu
from jax.sharding import PartitionSpec as P

NSTEP = 6
SIGMA_MAX = 4.0
SIGMA_MIN = 0.25
PLAN_POWER = 7.0
SECTIONS = 2
REACH = 8
PLANE = 4
VMEM_LIMIT = 40 * 1024 * 1024


def sigma_table(step_count):
    upper_root = SIGMA_MAX ** (1.0 / PLAN_POWER)
    lower_root = SIGMA_MIN ** (1.0 / PLAN_POWER)
    values = []
    for position in range(step_count):
        fraction = position / (step_count - 1)
        values.append((upper_root + fraction * (lower_root - upper_root)) ** PLAN_POWER)
    values.append(0.0)
    return values


def step_table():
    sigmas = sigma_table(NSTEP)
    steps = []
    for now, after in zip(sigmas[:-1], sigmas[1:]):
        scale = 1.0 / math.sqrt(now * now + 1.0)
        skip = 1.0 / (now * now + 1.0)
        rate = (after - now) / now
        steps.append((scale, 1.0 + rate * (1.0 - skip), -rate * now * scale))
    return sigmas[0], steps


def half_silu(half):
    return (half * jnp.tanh(half) + half).astype(jnp.bfloat16)


def dot(left, right):
    return jnp.dot(left, right, preferred_element_type=jnp.float32)


def halved(weight):
    return (0.5 * weight.astype(jnp.float32)).astype(jnp.bfloat16)


def dot_rows(left, right):
    return lax.dot_general(
        left, right, (((0,), (0,)), ((), ())), preferred_element_type=jnp.float32
    )


def denoise(noise, condition, w_in, w_mid, w_out):
    start, steps = step_table()
    latent = start * noise
    for scale, keep, gain in steps:
        stacked = jnp.concatenate([(scale * latent).astype(jnp.bfloat16), condition], axis=0)
        hidden = half_silu(dot_rows(w_in, stacked))
        hidden = half_silu(dot(w_mid, hidden))
        latent = keep * latent + gain * dot(w_out, hidden)
    return condition.astype(jnp.float32) + latent


def flat(field):
    return field.astype(jnp.float32).reshape(field.shape[0], -1)


def regress_kernel(coarse_ref, edge_ref, lift_ref, conv_ref, out_ref, condition_ref):
    section = lax.axis_index("section")
    channels_in, rows_all, width = coarse_ref.shape
    rows = rows_all // SECTIONS
    coarse = coarse_ref[...].astype(jnp.float32)
    edge = edge_ref[...].astype(jnp.float32)
    upper = jnp.concatenate([edge, coarse[:, : rows + 1]], axis=1)
    lower = jnp.concatenate([coarse[:, rows - 1 :], edge], axis=1)
    window = jnp.where(section == 0, upper, lower)
    window = window.reshape(channels_in, (rows + 2) * width).astype(jnp.bfloat16)
    half = dot_rows(halved(lift_ref[...]), window)
    lifted = half * jnp.tanh(half) + half
    channels = lifted.shape[0]
    column = lax.broadcasted_iota(jnp.int32, (channels, width), 1)
    taps = []
    for row in range(rows + 2):
        piece = lifted[:, row * width : (row + 1) * width]
        left = jnp.where(column == 0, 0.0, pltpu.roll(piece, 1, 1))
        right = jnp.where(column == width - 1, 0.0, pltpu.roll(piece, width - 1, 1))
        taps.append(jnp.concatenate([left, piece, right], axis=0).astype(jnp.bfloat16))
    stacked = jnp.concatenate(taps, axis=1)
    half = None
    for tap in range(3):
        weight = halved(conv_ref[tap].reshape(3 * channels, channels))
        part = dot_rows(weight, stacked[:, tap * width : (tap + rows) * width])
        half = part if half is None else half + part
    condition_ref[...] = dot(out_ref[...], half_silu(half)).astype(jnp.bfloat16)


def base_kernel(noise_ref, condition_ref, in_ref, mid_ref, out_ref, sums_ref):
    section = lax.axis_index("section")
    members, channels, rows_all, width = noise_ref.shape
    rows = rows_all // SECTIONS
    condition = condition_ref[...]
    noise = []
    for member in range(members):
        upper = noise_ref[member, :, :rows]
        lower = noise_ref[member, :, rows:]
        noise.append(flat(jnp.where(section == 0, upper, lower)))
    samples = denoise(
        jnp.concatenate(noise, axis=1),
        jnp.concatenate([condition] * members, axis=1),
        halved(in_ref[...]),
        halved(mid_ref[...]),
        out_ref[...],
    )
    cells = rows * width
    pieces = [samples[:, m * cells : (m + 1) * cells] for m in range(members)]
    sums_ref[0] = functools.reduce(lambda a, b: a + b, pieces)
    sums_ref[1] = functools.reduce(lambda a, b: a + b, [p * p for p in pieces])


def slot_plan(rows, tile, tiles, slots, ring):
    first = tile - lax.rem(tile, PLANE)
    lane = lax.broadcasted_iota(jnp.int32, rows[0][1].shape, 1)
    weight = jnp.zeros(lane.shape, jnp.float32)
    for step in range(5):
        weight = jnp.where(lane == lax.rem(tile + 2 * step, tiles), float(8**step), weight)
    plans = []
    for target in (tile, tile + 1 - 2 * lax.rem(tile, 2)):
        live = jnp.zeros(lane.shape, jnp.float32)
        rank = jnp.zeros(lane.shape, jnp.float32)
        for source, row in rows:
            live += (source == target).astype(jnp.float32) * row
            share = (source < target).astype(jnp.float32)
            if ring:
                share = jnp.where(first == 0, share, -(source > target).astype(jnp.float32))
            rank += share * row
        if ring:
            rank += jnp.where(first == 0, 0.0, slots - 1.0)
        packed = jnp.sum(weight * live * (rank + 1.0))
        plans.append((packed.astype(jnp.int32), jnp.sum(live)))
    return plans


def slot_kernel(*refs, members, slots, ring):
    if ring:
        behind_ref = None
    else:
        behind_ref, *refs = refs
    (
        plane_ref,
        plane4_ref,
        plane8_ref,
        mine_ref,
        theirs_ref,
        base_ref,
        in_ref,
        mid_ref,
        out_ref,
        own_ref,
        peer_ref,
        noise_ref,
        sample_ref,
        where_ref,
    ) = refs
    planes = (plane_ref, plane4_ref, plane8_ref)
    tile, tiles = lax.axis_index("tile"), lax.axis_size("tile")
    leading = lax.rem(tile, PLANE) < 2
    channels, cells = mine_ref.shape
    rows, width = noise_ref.shape[2:]
    blocks = plane_ref.shape[0] // 2
    chip = tile - lax.rem(tile, 2)
    other_chip = jnp.where(leading, chip + 2, chip - 2)
    names = []
    for ahead, plane in enumerate(planes):
        for start, last in ((chip, blocks - 1), (other_chip, 2 * blocks - 1)):
            block = plane[last].astype(jnp.float32)
            for odd in range(2):
                source = lax.rem(start + PLANE * ahead + odd, tiles)
                names.append((source, block[odd : odd + 1]))
    if not ring:
        block = behind_ref[...].astype(jnp.float32)
        for at in range(2 * PLANE):
            source = tile - lax.rem(tile, PLANE) + at - 2 * PLANE
            names.append((jnp.where(source < 0, source + tiles, source), block[at : at + 1]))
    plans = slot_plan(names, tile, tiles, slots, ring)

    def noise_of(step, slot):
        start = channels * slot
        if step % 2 == 0:
            return planes[step // 2][pl.ds(start, channels)]
        start = blocks + start
        near = planes[step // 2][pl.ds(start, channels)]
        far = planes[step // 2 + 1][pl.ds(start, channels)]
        return jnp.where(leading, near, far)

    count = jnp.int32(0)
    for side, (packed, _) in enumerate(plans):
        for step in range(5):
            digit = lax.shift_right_logical(packed, 3 * step) & 7

            noise_ref[count] = noise_of(step, jnp.maximum(digit - 1, 0))
            where_ref[count] = side
            count = count + (digit > 0).astype(jnp.int32)

    own_scale, peer_scale = [1.0 / (members + extra) for _, extra in plans]
    sample_ref[0] = base_ref[...]
    sample_ref[1] = jnp.zeros_like(base_ref)
    w_in, w_mid, w_out = halved(in_ref[...]), halved(mid_ref[...]), out_ref[...]

    def run(first, group):
        noise, conditions, sides = [], [], []
        for member in range(group):
            side = where_ref[first + member]
            sides.append(side)
            noise.append(flat(noise_ref[first + member]))
            conditions.append(jnp.where(side == 0, mine_ref[...], theirs_ref[...]))
        samples = denoise(
            jnp.concatenate(noise, axis=1), jnp.concatenate(conditions, axis=1), w_in, w_mid, w_out
        )
        for member in range(group):
            sample = samples[:, member * cells : (member + 1) * cells]
            sample_ref[sides[member], 0] += sample
            sample_ref[sides[member], 1] += sample * sample

    fours = count // 4
    left = count - 4 * fours

    @pl.loop(0, fours)
    def _(turn):
        run(4 * turn, 4)

    @pl.when(left >= 2)
    def _():
        run(4 * fours, 2)

    @pl.when((left & 1) == 1)
    def _():
        run(count - 1, 1)

    for moment in range(2):
        own_ref[moment] = (own_scale * sample_ref[0, moment]).reshape(channels, rows, width)
        peer_ref[moment] = (peer_scale * sample_ref[1, moment]).reshape(channels, rows, width)


def in_vmem(count):
    return [pl.BlockSpec(memory_space=pltpu.VMEM)] * count


def from_ahead(block, distance):
    count = lax.axis_size("tile")
    return lax.ppermute(block, "tile", [((i + distance) % count, i) for i in range(count)])


def swap_cores(block):
    count = lax.axis_size("tile")
    return lax.ppermute(block, "tile", [(i, i ^ 1) for i in range(count)])


def swap_chips(block):
    count = lax.axis_size("tile")
    return lax.ppermute(block, "tile", [(i, i ^ 2) for i in range(count)])


def swap_sections(block):
    return lax.ppermute(block, "section", [(0, 1), (1, 0)])


def send_edges(rows):
    count = lax.axis_size("tile")
    pairs = [(t, t + 1) for t in range(count - 1)]
    pairs += [(count + t + 1, count + t) for t in range(count - 1)]
    return lax.ppermute(rows, ("section", "tile"), pairs)


def body(
    coarse,
    lift_weight,
    conv_weight,
    out_weight,
    denoise_in,
    denoise_mid,
    denoise_out,
    base_noise,
    slot_noise,
    extra_dest,
):
    section = lax.axis_index("section")
    tile = lax.axis_index("tile")
    count = lax.axis_size("tile")
    slots, channels, rows_all, width = slot_noise.shape
    members = base_noise.shape[0]
    rows = rows_all // SECTIONS
    cells = rows * width
    hidden = denoise_mid.shape[0]
    step_flops = 2 * NSTEP * hidden * (hidden + 3 * channels)
    params = pltpu.CompilerParams(vmem_limit_bytes=VMEM_LIMIT)

    peer_routes = swap_cores(extra_dest)
    edge = jnp.where(section == 0, coarse[:, -1:], coarse[:, :1])
    edge, extra_dest, conv_weight, denoise_out, peer_routes = lax.optimization_barrier(
        (edge, extra_dest, conv_weight, denoise_out, peer_routes)
    )
    edge = send_edges(edge)
    conv_weight, denoise_out = swap_cores(conv_weight), swap_cores(denoise_out)
    even = jnp.where(tile % 2 == 0, extra_dest, peer_routes)
    odd = jnp.where(tile % 2 == 0, peer_routes, extra_dest)
    chip_routes = jnp.concatenate([even, odd], axis=0)
    devices = jnp.arange(width, dtype=jnp.int32)
    names = jnp.any(chip_routes[:, :, None] == devices, axis=1).astype(jnp.bfloat16)
    half_noise = lax.dynamic_slice_in_dim(slot_noise, rows * section, rows, axis=2)
    half_noise = half_noise.reshape(slots * channels, rows, width)
    block = jnp.pad(names, ((0, rows - 2), (0, 0)))
    record = jnp.concatenate([half_noise, block[None]], axis=0)
    across = swap_chips(record)

    condition = pl.pallas_call(
        regress_kernel,
        out_shape=jax.ShapeDtypeStruct((channels, cells), jnp.bfloat16),
        in_specs=in_vmem(5),
        out_specs=pl.BlockSpec(memory_space=pltpu.VMEM),
        compiler_params=params,
        cost_estimate=pl.CostEstimate(
            flops=2 * cells * hidden * (9 * hidden + 16),
            bytes_accessed=600_000,
            transcendentals=2 * cells * hidden,
        ),
        name="regression",
    )(coarse, edge, lift_weight.T, conv_weight, out_weight)

    plane = jnp.concatenate([record, across], axis=0)
    plane4, plane8 = from_ahead(plane, PLANE), from_ahead(plane, 2 * PLANE)
    peer_condition = swap_cores(condition)
    ring = count == 2 * REACH
    behind = []
    if not ring:
        leading = tile % PLANE < 2
        here, there = names, across[-1, :2]
        chips = [jnp.where(leading, here, there), jnp.where(leading, there, here)]
        chips = jnp.concatenate(chips, axis=0)
        chips = [from_ahead(chips, -2 * PLANE), from_ahead(chips, -PLANE)]
        behind = [jnp.pad(jnp.concatenate(chips, axis=0), ((0, rows - 2 * PLANE), (0, 0)))]

    base = pl.pallas_call(
        base_kernel,
        out_shape=jax.ShapeDtypeStruct((2, channels, cells), jnp.float32),
        in_specs=in_vmem(5),
        out_specs=pl.BlockSpec(memory_space=pltpu.VMEM),
        compiler_params=params,
        cost_estimate=pl.CostEstimate(
            flops=members * cells * step_flops,
            bytes_accessed=400_000,
            transcendentals=2 * NSTEP * members * cells * hidden,
        ),
        name="base_members",
    )(base_noise, condition, denoise_in.T, denoise_mid, denoise_out)

    moments = jax.ShapeDtypeStruct((2, channels, rows, width), jnp.float32)
    own, peer = pl.pallas_call(
        functools.partial(slot_kernel, members=members, slots=slots, ring=ring),
        out_shape=(moments, moments),
        in_specs=in_vmem(9 + len(behind)),
        out_specs=(pl.BlockSpec(memory_space=pltpu.VMEM),) * 2,
        scratch_shapes=[
            pltpu.VMEM((12, channels, rows, width), jnp.bfloat16),
            pltpu.VMEM((2, 2, channels, cells), jnp.float32),
            pltpu.SMEM((12,), jnp.int32),
        ],
        compiler_params=params,
        cost_estimate=pl.CostEstimate(
            flops=slots * cells * step_flops,
            bytes_accessed=1_000_000,
            transcendentals=2 * NSTEP * slots * cells * hidden,
        ),
        name="slot_members",
    )(
        *behind,
        plane,
        plane4,
        plane8,
        condition,
        peer_condition,
        base,
        denoise_in.T,
        denoise_mid,
        denoise_out,
    )
    total = own + swap_cores(peer)
    mean = total[0]
    variance = total[1] - mean * mean
    kept = jnp.where(section == 0, mean, variance)
    sent = jnp.where(section == 0, variance, mean)
    received = swap_sections(sent)
    upper = jnp.where(section == 0, kept, received)
    lower = jnp.where(section == 0, received, kept)
    return jnp.concatenate([upper, lower], axis=1)[None]


def solution(mesh):
    in_specs = (
        P(None, "tile", None),
        P(),
        P(),
        P(),
        P(),
        P(),
        P(),
        P(None, None, "tile", None),
        P(None, None, "tile", None),
        P("tile", None),
    )
    out_specs = P("section", None, "tile", None)
    return jax.shard_map(body, mesh=mesh, in_specs=in_specs, out_specs=out_specs, check_vma=False)
```

```python
import functools
import math

import jax
import jax.numpy as jnp
from jax import lax
from jax.experimental import pallas as pl
from jax.experimental.pallas import tpu as pltpu
from jax.sharding import PartitionSpec as P

NSTEP = 6
SIGMA_MAX = 4.0
SIGMA_MIN = 0.25
PLAN_POWER = 7.0
SECTIONS = 2
REACH = 8
PLANE = 4
VMEM_LIMIT = 40 * 1024 * 1024


def sigma_table(step_count):
    upper_root = SIGMA_MAX ** (1.0 / PLAN_POWER)
    lower_root = SIGMA_MIN ** (1.0 / PLAN_POWER)
    values = []
    for position in range(step_count):
        fraction = position / (step_count - 1)
        values.append((upper_root + fraction * (lower_root - upper_root)) ** PLAN_POWER)
    values.append(0.0)
    return values


def step_table():
    sigmas = sigma_table(NSTEP)
    steps = []
    for now, after in zip(sigmas[:-1], sigmas[1:]):
        scale = 1.0 / math.sqrt(now * now + 1.0)
        skip = 1.0 / (now * now + 1.0)
        rate = (after - now) / now
        steps.append((scale, 1.0 + rate * (1.0 - skip), -rate * now * scale))
    return sigmas[0], steps


def half_silu(half):
    return (half * jnp.tanh(half) + half).astype(jnp.bfloat16)


def dot(left, right):
    return jnp.dot(left, right, preferred_element_type=jnp.float32)


def halved(weight):
    return (0.5 * weight.astype(jnp.float32)).astype(jnp.bfloat16)


def dot_rows(left, right):
    return lax.dot_general(
        left, right, (((0,), (0,)), ((), ())), preferred_element_type=jnp.float32
    )


def denoise(noise, condition, w_in, w_mid, w_out):
    start, steps = step_table()
    latent = start * noise
    for scale, keep, gain in steps:
        stacked = jnp.concatenate([(scale * latent).astype(jnp.bfloat16), condition], axis=0)
        hidden = half_silu(dot_rows(w_in, stacked))
        hidden = half_silu(dot(w_mid, hidden))
        latent = keep * latent + gain * dot(w_out, hidden)
    return condition.astype(jnp.float32) + latent


def flat(field):
    return field.astype(jnp.float32).reshape(field.shape[0], -1)


def regress_kernel(coarse_ref, edge_ref, lift_ref, conv_ref, out_ref, condition_ref):
    section = lax.axis_index("section")
    channels_in, rows_all, width = coarse_ref.shape
    rows = rows_all // SECTIONS
    coarse = coarse_ref[...].astype(jnp.float32)
    edge = edge_ref[...].astype(jnp.float32)
    upper = jnp.concatenate([edge, coarse[:, : rows + 1]], axis=1)
    lower = jnp.concatenate([coarse[:, rows - 1 :], edge], axis=1)
    window = jnp.where(section == 0, upper, lower)
    window = window.reshape(channels_in, (rows + 2) * width).astype(jnp.bfloat16)
    half = dot_rows(halved(lift_ref[...]), window)
    lifted = half * jnp.tanh(half) + half
    channels = lifted.shape[0]
    column = lax.broadcasted_iota(jnp.int32, (channels, width), 1)
    taps = []
    for row in range(rows + 2):
        piece = lifted[:, row * width : (row + 1) * width]
        left = jnp.where(column == 0, 0.0, pltpu.roll(piece, 1, 1))
        right = jnp.where(column == width - 1, 0.0, pltpu.roll(piece, width - 1, 1))
        taps.append(jnp.concatenate([left, piece, right], axis=0).astype(jnp.bfloat16))
    stacked = jnp.concatenate(taps, axis=1)
    half = None
    for tap in range(3):
        weight = halved(conv_ref[tap].reshape(3 * channels, channels))
        part = dot_rows(weight, stacked[:, tap * width : (tap + rows) * width])
        half = part if half is None else half + part
    condition_ref[...] = dot(out_ref[...], half_silu(half)).astype(jnp.bfloat16)


def base_kernel(noise_ref, condition_ref, in_ref, mid_ref, out_ref, sums_ref):
    section = lax.axis_index("section")
    members, channels, rows_all, width = noise_ref.shape
    rows = rows_all // SECTIONS
    condition = condition_ref[...]
    noise = []
    for member in range(members):
        upper = noise_ref[member, :, :rows]
        lower = noise_ref[member, :, rows:]
        noise.append(flat(jnp.where(section == 0, upper, lower)))
    samples = denoise(
        jnp.concatenate(noise, axis=1),
        jnp.concatenate([condition] * members, axis=1),
        halved(in_ref[...]),
        halved(mid_ref[...]),
        out_ref[...],
    )
    cells = rows * width
    pieces = [samples[:, m * cells : (m + 1) * cells] for m in range(members)]
    sums_ref[0] = functools.reduce(lambda a, b: a + b, pieces)
    sums_ref[1] = functools.reduce(lambda a, b: a + b, [p * p for p in pieces])


def slot_plan(rows, tile, tiles, slots, ring):
    first = tile - lax.rem(tile, PLANE)
    lane = lax.broadcasted_iota(jnp.int32, rows[0][1].shape, 1)
    weight = jnp.zeros(lane.shape, jnp.float32)
    for step in range(5):
        weight = jnp.where(lane == lax.rem(tile + 2 * step, tiles), float(8**step), weight)
    plans = []
    for target in (tile, tile + 1 - 2 * lax.rem(tile, 2)):
        live = jnp.zeros(lane.shape, jnp.float32)
        rank = jnp.zeros(lane.shape, jnp.float32)
        for source, row in rows:
            live += (source == target).astype(jnp.float32) * row
            share = (source < target).astype(jnp.float32)
            if ring:
                share = jnp.where(first == 0, share, -(source > target).astype(jnp.float32))
            rank += share * row
        if ring:
            rank += jnp.where(first == 0, 0.0, slots - 1.0)
        both = jnp.sum(live * (weight * (rank + 1.0) + float(8**5))).astype(jnp.int32)
        extra = lax.shift_right_logical(both, 15)
        plans.append((both & (8**5 - 1), extra.astype(jnp.float32)))
    return plans


def slot_kernel(*refs, members, slots, ring):
    if ring:
        behind_ref = None
    else:
        behind_ref, *refs = refs
    (
        plane_ref,
        plane4_ref,
        plane8_ref,
        mine_ref,
        theirs_ref,
        base_ref,
        in_ref,
        mid_ref,
        out_ref,
        own_ref,
        peer_ref,
        noise_ref,
        sample_ref,
        where_ref,
    ) = refs
    planes = (plane_ref, plane4_ref, plane8_ref)
    tile, tiles = lax.axis_index("tile"), lax.axis_size("tile")
    leading = lax.rem(tile, PLANE) < 2
    channels, cells = mine_ref.shape
    rows, width = noise_ref.shape[2:]
    blocks = plane_ref.shape[0] // 2
    chip = tile - lax.rem(tile, 2)
    other_chip = jnp.where(leading, chip + 2, chip - 2)
    names = []
    for ahead, plane in enumerate(planes):
        for start, last in ((chip, blocks - 1), (other_chip, 2 * blocks - 1)):
            block = plane[last].astype(jnp.float32)
            for odd in range(2):
                source = lax.rem(start + PLANE * ahead + odd, tiles)
                names.append((source, block[odd : odd + 1]))
    if not ring:
        block = behind_ref[...].astype(jnp.float32)
        for at in range(2 * PLANE):
            source = tile - lax.rem(tile, PLANE) + at - 2 * PLANE
            names.append((jnp.where(source < 0, source + tiles, source), block[at : at + 1]))
    plans = slot_plan(names, tile, tiles, slots, ring)

    def noise_of(step, slot):
        start = channels * slot
        if step % 2 == 0:
            return planes[step // 2][pl.ds(start, channels)]
        start = blocks + start
        near = planes[step // 2][pl.ds(start, channels)]
        far = planes[step // 2 + 1][pl.ds(start, channels)]
        return jnp.where(leading, near, far)

    count = jnp.int32(0)
    for side, (packed, _) in enumerate(plans):
        for step in range(5 - (side == 0)):
            digit = lax.shift_right_logical(packed, 3 * step) & 7

            noise_ref[count] = noise_of(step, jnp.maximum(digit - 1, 0))
            where_ref[count] = side
            count = count + (digit > 0).astype(jnp.int32)

    own_scale, peer_scale = [1.0 / (members + extra) for _, extra in plans]
    sample_ref[0] = base_ref[...]
    sample_ref[1] = jnp.zeros_like(base_ref)
    w_in, w_mid, w_out = halved(in_ref[...]), halved(mid_ref[...]), out_ref[...]

    def run(first, group):
        noise, conditions, sides = [], [], []
        for member in range(group):
            side = where_ref[first + member]
            sides.append(side)
            noise.append(flat(noise_ref[first + member]))
            conditions.append(jnp.where(side == 0, mine_ref[...], theirs_ref[...]))
        samples = denoise(
            jnp.concatenate(noise, axis=1), jnp.concatenate(conditions, axis=1), w_in, w_mid, w_out
        )
        for member in range(group):
            sample = samples[:, member * cells : (member + 1) * cells]
            sample_ref[sides[member], 0] += sample
            sample_ref[sides[member], 1] += sample * sample

    fours = count // 4
    left = count - 4 * fours

    @pl.loop(0, fours)
    def _(turn):
        run(4 * turn, 4)

    @pl.when(left >= 2)
    def _():
        run(4 * fours, 2)

    @pl.when((left & 1) == 1)
    def _():
        run(count - 1, 1)

    for moment in range(2):
        own_ref[moment] = (own_scale * sample_ref[0, moment]).reshape(channels, rows, width)
        peer_ref[moment] = (peer_scale * sample_ref[1, moment]).reshape(channels, rows, width)


def in_vmem(count):
    return [pl.BlockSpec(memory_space=pltpu.VMEM)] * count


def from_ahead(block, distance):
    count = lax.axis_size("tile")
    return lax.ppermute(block, "tile", [((i + distance) % count, i) for i in range(count)])


def swap_cores(block):
    count = lax.axis_size("tile")
    return lax.ppermute(block, "tile", [(i, i ^ 1) for i in range(count)])


def swap_chips(block):
    count = lax.axis_size("tile")
    return lax.ppermute(block, "tile", [(i, i ^ 2) for i in range(count)])


def swap_sections(block):
    return lax.ppermute(block, "section", [(0, 1), (1, 0)])


def send_edges(rows):
    count = lax.axis_size("tile")
    pairs = [(t, t + 1) for t in range(count - 1)]
    pairs += [(count + t + 1, count + t) for t in range(count - 1)]
    return lax.ppermute(rows, ("section", "tile"), pairs)


def body(
    coarse,
    lift_weight,
    conv_weight,
    out_weight,
    denoise_in,
    denoise_mid,
    denoise_out,
    base_noise,
    slot_noise,
    extra_dest,
):
    section = lax.axis_index("section")
    tile = lax.axis_index("tile")
    count = lax.axis_size("tile")
    slots, channels, rows_all, width = slot_noise.shape
    members = base_noise.shape[0]
    rows = rows_all // SECTIONS
    cells = rows * width
    hidden = denoise_mid.shape[0]
    step_flops = 2 * NSTEP * hidden * (hidden + 3 * channels)
    params = pltpu.CompilerParams(vmem_limit_bytes=VMEM_LIMIT)

    peer_routes = swap_cores(extra_dest)
    edge = jnp.where(section == 0, coarse[:, -1:], coarse[:, :1])
    edge, extra_dest, conv_weight, denoise_out, peer_routes = lax.optimization_barrier(
        (edge, extra_dest, conv_weight, denoise_out, peer_routes)
    )
    edge = send_edges(edge)
    conv_weight, denoise_out = swap_cores(conv_weight), swap_cores(denoise_out)
    even = jnp.where(tile % 2 == 0, extra_dest, peer_routes)
    odd = jnp.where(tile % 2 == 0, peer_routes, extra_dest)
    chip_routes = jnp.concatenate([even, odd], axis=0)
    devices = jnp.arange(width, dtype=jnp.int32)
    names = jnp.any(chip_routes[:, :, None] == devices, axis=1).astype(jnp.bfloat16)
    half_noise = lax.dynamic_slice_in_dim(slot_noise, rows * section, rows, axis=2)
    half_noise = half_noise.reshape(slots * channels, rows, width)
    block = jnp.pad(names, ((0, rows - 2), (0, 0)))
    record = jnp.concatenate([half_noise, block[None]], axis=0)
    across = swap_chips(record)

    condition = pl.pallas_call(
        regress_kernel,
        out_shape=jax.ShapeDtypeStruct((channels, cells), jnp.bfloat16),
        in_specs=in_vmem(5),
        out_specs=pl.BlockSpec(memory_space=pltpu.VMEM),
        compiler_params=params,
        cost_estimate=pl.CostEstimate(
            flops=2 * cells * hidden * (9 * hidden + 16),
            bytes_accessed=600_000,
            transcendentals=2 * cells * hidden,
        ),
        name="regression",
    )(coarse, edge, lift_weight.T, conv_weight, out_weight)

    plane = jnp.concatenate([record, across], axis=0)
    plane4, plane8 = from_ahead(plane, PLANE), from_ahead(plane, 2 * PLANE)
    peer_condition = swap_cores(condition)
    ring = count == 2 * REACH
    behind = []
    if not ring:
        leading = tile % PLANE < 2
        here, there = names, across[-1, :2]
        chips = [jnp.where(leading, here, there), jnp.where(leading, there, here)]
        chips = jnp.concatenate(chips, axis=0)
        chips = [from_ahead(chips, -2 * PLANE), from_ahead(chips, -PLANE)]
        behind = [jnp.pad(jnp.concatenate(chips, axis=0), ((0, rows - 2 * PLANE), (0, 0)))]

    base = pl.pallas_call(
        base_kernel,
        out_shape=jax.ShapeDtypeStruct((2, channels, cells), jnp.float32),
        in_specs=in_vmem(5),
        out_specs=pl.BlockSpec(memory_space=pltpu.VMEM),
        compiler_params=params,
        cost_estimate=pl.CostEstimate(
            flops=members * cells * step_flops,
            bytes_accessed=400_000,
            transcendentals=2 * NSTEP * members * cells * hidden,
        ),
        name="base_members",
    )(base_noise, condition, denoise_in.T, denoise_mid, denoise_out)

    moments = jax.ShapeDtypeStruct((2, channels, rows, width), jnp.float32)
    own, peer = pl.pallas_call(
        functools.partial(slot_kernel, members=members, slots=slots, ring=ring),
        out_shape=(moments, moments),
        in_specs=in_vmem(9 + len(behind)),
        out_specs=(pl.BlockSpec(memory_space=pltpu.VMEM),) * 2,
        scratch_shapes=[
            pltpu.VMEM((12, channels, rows, width), jnp.bfloat16),
            pltpu.VMEM((2, 2, channels, cells), jnp.float32),
            pltpu.SMEM((12,), jnp.int32),
        ],
        compiler_params=params,
        cost_estimate=pl.CostEstimate(
            flops=slots * cells * step_flops,
            bytes_accessed=1_000_000,
            transcendentals=2 * NSTEP * slots * cells * hidden,
        ),
        name="slot_members",
    )(
        *behind,
        plane,
        plane4,
        plane8,
        condition,
        peer_condition,
        base,
        denoise_in.T,
        denoise_mid,
        denoise_out,
    )
    total = own + swap_cores(peer)
    mean = total[0]
    variance = total[1] - mean * mean
    kept = jnp.where(section == 0, mean, variance)
    sent = jnp.where(section == 0, variance, mean)
    received = swap_sections(sent)
    upper = jnp.where(section == 0, kept, received)
    lower = jnp.where(section == 0, received, kept)
    return jnp.concatenate([upper, lower], axis=1)[None]


def solution(mesh):
    in_specs = (
        P(None, "tile", None),
        P(),
        P(),
        P(),
        P(),
        P(),
        P(),
        P(None, None, "tile", None),
        P(None, None, "tile", None),
        P("tile", None),
    )
    out_specs = P("section", None, "tile", None)
    return jax.shard_map(body, mesh=mesh, in_specs=in_specs, out_specs=out_specs, check_vma=False)
```
